128 devices in a mesh: section: 4 (over z), replica: 32 (over y, x, core).
Axes of the slice: x: 4, y: 4, z: 4, core: 2. Of those that a mesh axis runs over, the one named last changes fastest.
Arguments:
- images: bfloat16 [4, 32, 12, 12, 1024], P(None, 'replica'), may hold values from -6 to 6
- cotangent: bfloat16 [4, 32, 12, 12, 1024], P(None, 'replica'), may hold values from -6 to 6
- depth_first: bfloat16 [4, 9, 1024], P('section'), may hold values from -3 to 3
- point_first: bfloat16 [4, 1024, 1024], P('section'), may hold values from -0.1875 to 0.1875
- depth_second: bfloat16 [4, 9, 1024], P('section'), may hold values from -3 to 3
- point_second: bfloat16 [4, 1024, 1024], P('section'), may hold values from -0.1875 to 0.1875
Outputs:
- grad_depth_first: float32 [4, 9, 1024], P('section')
- grad_point_first: float32 [4, 1024, 1024], P('section')
- grad_depth_second: float32 [4, 9, 1024], P('section')
- grad_point_second: float32 [4, 1024, 1024], P('section')
The draws below stay inside these ranges and needn't reach their ends.
All inputs are finite; a program needn't handle non-finite values.
Results may differ from the reference program's by a relative error of at most 0.04.
Values may be sent and summed in bfloat16 or wider, within the bound.
No kernel may reach another device: no remote copies, remote signals or barrier semaphores. Data moves between devices by JAX's collectives and lax.ppermute only.
A program may use at most 192 MiB of HBM per device.

```python
import jax
import jax.numpy as jnp
from jax import lax

C = 1024
SIDE = 12
MICRO = 4
SECTIONS = 4
BATCH = 32


def shard_levels(rng, extent, cuts, least, top_value):
    def one(position, shards_of):
        draws = jax.random.uniform(jax.random.fold_in(jax.random.fold_in(rng, 6), position), (shards_of,), jnp.float32, least / len(cuts), top_value / len(cuts))
        return jnp.repeat(jnp.exp(draws), extent[position] // shards_of).reshape((-1,) + (1,) * (len(extent) - position - 1))

    loudness = one(*cuts[0])
    for cut in cuts[1:]:
        loudness = loudness * one(*cut)
    return loudness


def gaussian(rng, shape, spread, most, shards=(), kind=jnp.bfloat16):
    entries = spread * jax.random.normal(rng, shape, jnp.float32)
    if shards:
        entries = entries * shard_levels(rng, shape, shards, -0.22, 0.18)
    return jnp.clip(entries, -most, most).astype(kind)


def setup_inputs(seed: int = 0) -> dict:
    splits = jax.random.split(jax.random.key(seed), 7)
    images = gaussian(splits[0], (MICRO, BATCH, SIDE, SIDE, C), 1.0, 6.0, ((1, 32),))
    cotangent = gaussian(splits[1], (MICRO, BATCH, SIDE, SIDE, C), 1.0, 6.0, ((1, 32),))
    depth_first = gaussian(splits[2], (SECTIONS, 9, C), 4 ** -0.5, 3.0, ((0, 4),))
    point_first = gaussian(splits[3], (SECTIONS, C, C), C ** -0.5, 0.1875, ((0, 4),))
    depth_second = gaussian(splits[4], (SECTIONS, 9, C), 4 ** -0.5, 3.0, ((0, 4),))
    point_second = gaussian(splits[5], (SECTIONS, C, C), C ** -0.5, 0.1875, ((0, 4),))
    return {"images": images, "cotangent": cotangent, "depth_first": depth_first, "point_first": point_first, "depth_second": depth_second, "point_second": point_second}


def tap_shift(field, row_off, col_off):
    height, width = (field.shape[1], field.shape[2])
    padded = jnp.pad(field, ((0, 0), (2, 2), (2, 2), (0, 0)))
    return padded[:, 2 + row_off:2 + row_off + height, 2 + col_off:2 + col_off + width, :]

def depthwise(field, kernel, dilation, direction):
    running = jnp.zeros_like(field)
    for number in range(9):
        row_off = (number // 3 - 1) * dilation * direction
        col_off = (number % 3 - 1) * dilation * direction
        running = running + kernel[number] * tap_shift(field, row_off, col_off)
    return running

def kernel_grad(field, outgrad, dilation):
    layers = []
    for number in range(9):
        row_off = (number // 3 - 1) * dilation
        col_off = (number % 3 - 1) * dilation
        layers.append(lax.optimization_barrier(jnp.sum(tap_shift(field, row_off, col_off) * outgrad, axis=(0, 1, 2))))
    return jnp.stack(layers)

def silu_slope(value):
    sigma = jax.nn.sigmoid(value)
    return sigma * (1.0 + value * (1.0 - sigma))

def flatten_rows(array):
    return array.reshape(-1, array.shape[-1])

def section_forward(inflow, weights):
    depth_one, point_one, depth_two, point_two = weights
    smoothed = jax.nn.silu(inflow.astype(jnp.float32))
    first_conv = depthwise(smoothed, depth_one.astype(jnp.float32), 1, 1).astype(jnp.bfloat16)
    pre_float = jnp.dot(flatten_rows(first_conv), point_one, preferred_element_type=jnp.float32)
    projected = pre_float.astype(jnp.bfloat16).reshape(inflow.shape)
    hidden = jax.nn.silu(pre_float).astype(jnp.bfloat16).reshape(inflow.shape)
    second_conv = depthwise(hidden.astype(jnp.float32), depth_two.astype(jnp.float32), 2, 1).astype(jnp.bfloat16)
    branch = jnp.dot(flatten_rows(second_conv), point_two, preferred_element_type=jnp.float32).reshape(inflow.shape)
    outflow = (inflow.astype(jnp.float32) + branch).astype(jnp.bfloat16)
    return (outflow, (first_conv, projected, hidden, second_conv))

def section_backward(inflow, interior, outgrad, weights):
    depth_one, point_one, depth_two, point_two = weights
    first_conv, projected, hidden, second_conv = interior
    out_rows = flatten_rows(outgrad)
    grad_point_two = jnp.dot(flatten_rows(second_conv).T, out_rows, preferred_element_type=jnp.float32)
    grad_second = jnp.dot(out_rows, point_two.T, preferred_element_type=jnp.float32).astype(jnp.bfloat16).reshape(inflow.shape)
    grad_depth_two = kernel_grad(hidden.astype(jnp.float32), grad_second.astype(jnp.float32), 2)
    grad_hidden = depthwise(grad_second.astype(jnp.float32), depth_two.astype(jnp.float32), 2, -1)
    grad_projected = (grad_hidden * silu_slope(projected.astype(jnp.float32))).astype(jnp.bfloat16)
    projected_rows = flatten_rows(grad_projected)
    grad_point_one = jnp.dot(flatten_rows(first_conv).T, projected_rows, preferred_element_type=jnp.float32)
    grad_first = jnp.dot(projected_rows, point_one.T, preferred_element_type=jnp.float32).astype(jnp.bfloat16).reshape(inflow.shape)
    inflow_float = inflow.astype(jnp.float32)
    smoothed = jax.nn.silu(inflow_float)
    grad_depth_one = kernel_grad(smoothed, grad_first.astype(jnp.float32), 1)
    grad_smoothed = depthwise(grad_first.astype(jnp.float32), depth_one.astype(jnp.float32), 1, -1)
    ingrad = (outgrad.astype(jnp.float32) + grad_smoothed * silu_slope(inflow_float)).astype(jnp.bfloat16)
    return (ingrad, (grad_depth_one, grad_point_one, grad_depth_two, grad_point_two))

def reference(images, cotangent, depth_first, point_first, depth_second, point_second):
    section_count = depth_first.shape[0]
    totals = [[jnp.zeros(array.shape[1:], jnp.float32) for array in (depth_first, point_first, depth_second, point_second)] for section_number in range(section_count)]
    for micro_index in range(MICRO):
        inputs = []
        moving = images[micro_index]
        for section_number in range(section_count):
            weights = (depth_first[section_number], point_first[section_number], depth_second[section_number], point_second[section_number])
            inputs.append(moving)
            moving = section_forward(moving, weights)[0]
        returning = cotangent[micro_index]
        for section_number in reversed(range(section_count)):
            weights = (depth_first[section_number], point_first[section_number], depth_second[section_number], point_second[section_number])
            interior = section_forward(inputs[section_number], weights)[1]
            returning, contribs = section_backward(inputs[section_number], interior, returning, weights)
            totals[section_number] = [running + contrib for running, contrib in zip(totals[section_number], contribs)]
    return (jnp.stack([row[0] for row in totals]), jnp.stack([row[1] for row in totals]), jnp.stack([row[2] for row in totals]), jnp.stack([row[3] for row in totals]))
```

```python
import functools
from types import SimpleNamespace

import jax
import jax.numpy as jnp
from jax import lax
from jax.experimental import pallas as pl
from jax.experimental.pallas import tpu as pltpu
from jax.sharding import PartitionSpec as P

BF = jnp.bfloat16
F32 = jnp.float32
SIDE = 12
ROWS = SIDE * SIDE
C = 1024
GROUPS = C // 128
LINE = SIDE * GROUPS
MICRO = 4
SECTIONS = 4
MAP1 = (SIDE + 2) * LINE
MAP2 = (SIDE + 4) * LINE
FLAT = SIDE * LINE
MIB = 1024 * 1024
SECTION = "section"
REPLICA = "replica"

ANY = pl.BlockSpec(memory_space=pl.ANY)
VM = pl.BlockSpec(memory_space=pltpu.VMEM)


def sigmoid(v):
    return 0.5 * jnp.tanh(0.5 * v) + 0.5


def slope(v):
    s = sigmoid(v)
    return s * (1.0 + v * (1.0 - s))


def widen_kernel(k_ref, wide):
    for g in range(GROUPS):
        wide[pl.ds(g, 9, stride=GROUPS), :] = k_ref[:, 128 * g : 128 * (g + 1)].astype(F32)


def clear_edges(field, dilation):
    size = dilation * LINE
    zero = jnp.zeros((size, 128), F32)
    field[pl.ds(0, size), :] = zero
    field[pl.ds(FLAT + size, size), :] = zero


def depthwise(field, wide, out, dilation, flip):
    taps = [wide[pl.ds(8 * (8 - t if flip else t), 8), :] for t in range(9)]

    def line(i, carry):
        seen = {}

        def at(p, j):
            if (p, j) not in seen:
                start = pl.multiple_of((i + p * dilation) * LINE + j * GROUPS, 8)
                seen[p, j] = field[pl.ds(start, 8), :]
            return seen[p, j]

        for j in range(SIDE):
            total = None
            for t in range(9):
                p, q = divmod(t, 3)
                col = j + (q - 1) * dilation
                if 0 <= col < SIDE:
                    term = taps[t] * at(p, col)
                    total = term if total is None else total + term
            out[pl.ds(pl.multiple_of(i * LINE + j * GROUPS, 8), 8), :] = total
        return carry

    lax.fori_loop(0, SIDE, line, 0)


def kernel_grad(field, grad, dilation):
    def line(i, sums):
        sums = list(sums)
        seen = {}

        def at(p, j):
            if (p, j) not in seen:
                start = pl.multiple_of((i + p * dilation) * LINE + j * GROUPS, 8)
                seen[p, j] = field[pl.ds(start, 8), :]
            return seen[p, j]

        for j in range(SIDE):
            here = grad[pl.ds(pl.multiple_of((i + dilation) * LINE + j * GROUPS, 8), 8), :]
            for t in range(9):
                p, q = divmod(t, 3)
                col = j + (q - 1) * dilation
                if 0 <= col < SIDE:
                    sums[t] = sums[t] + here * at(p, col)
        return tuple(sums)

    return lax.fori_loop(0, SIDE, line, tuple(jnp.zeros((8, 128), F32) for _ in range(9)))


def rows_to_map(field, base, p, g, value):
    field[pl.ds(base + 16 * p * GROUPS + g, 16, stride=GROUPS), :] = value


def map_to_rows(field, p, g):
    return field[pl.ds(16 * p * GROUPS + g, 16, stride=GROUPS), :]


def tiles(body):
    def step(p, carry):
        for g in range(GROUPS):
            body(p, g, pl.ds(pl.multiple_of(16 * p, 16), 16), pl.ds(128 * g, 128))
        return carry

    lax.fori_loop(0, ROWS // 16, step, 0)


def dot(a, b, dims):
    return lax.dot_general(a, b, (dims, ((), ())), preferred_element_type=F32)


def rows_type(n=ROWS):
    return jax.ShapeDtypeStruct((n, C), BF)


def map_type(n):
    return jax.ShapeDtypeStruct((n, 128), F32)


def call(body, ins, outs, scratch, limit, name, flops, size, aliases=None):
    flat, tree = jax.tree.flatten(ins)
    out_flat, out_tree = jax.tree.flatten(outs)

    def kernel(*refs):
        first, last = len(flat), len(flat) + len(out_flat)
        given = SimpleNamespace(**jax.tree.unflatten(tree, refs[:first]))
        made = SimpleNamespace(**jax.tree.unflatten(out_tree, refs[first:last]))
        body(given, made, refs[last:])

    def names(arrays):
        return jax.tree.leaves({n: jax.tree.map(lambda _: n, value) for n, value in arrays.items()})

    def specs(arrays):
        return [ANY if n.startswith("_") else VM for n in names(arrays)]

    found = pl.pallas_call(
        kernel,
        out_shape=out_flat,
        in_specs=specs(ins),
        out_specs=specs(outs),
        scratch_shapes=scratch,
        input_output_aliases={
            names(ins).index(a): names(outs).index(b) for a, b in (aliases or {}).items()
        },
        compiler_params=pltpu.CompilerParams(vmem_limit_bytes=limit * MIB),
        cost_estimate=pl.CostEstimate(flops=flops, bytes_accessed=size, transcendentals=0),
        name=name,
    )(*flat)
    return SimpleNamespace(**jax.tree.unflatten(out_tree, found))


class Copies:
    def __init__(self, sems):
        self.sems = sems
        self.count = 0

    def next(self):
        self.count += 1
        return self.sems.at[self.count - 1]

    def start(self, source, target):
        copy = pltpu.make_async_copy(source, target, self.next())
        copy.start()
        return copy

    def by_section(self, section, choices, target):
        sem = self.next()
        for s, source in choices.items():

            @pl.when(section == s)
            def _(source=source):
                pltpu.make_async_copy(source, target, sem).start()

        return pltpu.make_async_copy(target, target, sem)

    def by_core(self, core, value, on_zero, on_one):
        sem = self.next()

        @pl.when(core == 0)
        def _():
            pltpu.make_async_copy(value, on_zero, sem).start()

        @pl.when(core == 1)
        def _():
            pltpu.make_async_copy(value, on_one, sem).start()

        return pltpu.make_async_copy(value, value, sem)


def this_core():
    return lax.rem(lax.axis_index(REPLICA), 2)


def rows_scratch(n=ROWS):
    return pltpu.VMEM((n, C), BF)


def map_scratch(n):
    return pltpu.VMEM((n, 128), F32)


def pick(section, target, choices):
    if len(choices) == 1:
        return next(iter(choices.values()))
    for s, ref in choices.items():

        @pl.when(section == s)
        def _(ref=ref):
            target[...] = ref[...]

    return target


def forward_sections(moment):
    return [s for s in range(SECTIONS) if 0 <= moment - s < MICRO]


def forward_body(moment, ins, outs, scratch):
    xs, wide1, wide2, map1, map2, work, fv, sv, pv, sems, *own = scratch
    section = lax.axis_index(SECTION)
    core = this_core()
    slot = moment - section

    @pl.when((slot >= 0) & (slot < MICRO))
    def _():
        copies = Copies(sems)
        x_out = outs.x
        if moment < MICRO:
            get_x = pltpu.make_async_copy(ins._images.at[moment], xs, copies.next())
            pl.when(section == 0)(get_x.start)
        puts = []
        if own:
            w1, w2 = own
            gets = [copies.start(ins._p1, w1), copies.start(ins._p2, w2)]
        else:
            w1, w2 = ins.p1, ins.p2
        widen_kernel(ins.k1, wide1)
        widen_kernel(ins.k2, wide2)
        clear_edges(map1, 1)
        clear_edges(map2, 2)
        if moment < MICRO:
            pl.when(section == 0)(get_x.wait)
        came = {s: ins.came[s % 2] for s in forward_sections(moment) if s > 0}
        if moment < MICRO and moment > 0:
            came[0] = xs
            for s, ref in came.items():
                if s > 0:

                    @pl.when(section == s)
                    def _(ref=ref):
                        xs[...] = ref[...]

        xv = xs if moment < MICRO else pick(section, xs, came)
        if moment > 0:
            puts.append(copies.start(xv, outs._x))

        def enter(p, g, rows, cols):
            v = xv[rows, cols].astype(F32)
            rows_to_map(map1, LINE, p, g, v * sigmoid(v))

        tiles(enter)
        depthwise(map1, wide1, work, 1, False)

        def collect_first(p, g, rows, cols):
            fv[rows, cols] = map_to_rows(work, p, g).astype(BF)

        tiles(collect_first)
        if own:
            for get in gets:
                get.wait()
        puts.append(copies.start(map1, outs._map1))
        puts.append(copies.by_core(core, fv, outs._keep, outs._send))
        for n in range(4):
            cols = pl.ds(256 * n, 256)
            pre = dot(fv[...], w1[:, cols], ((1,), (0,)))
            pv[:, cols] = pre.astype(BF)
            hidden = (pre * sigmoid(pre)).astype(BF).astype(F32)
            for g in range(2):
                map2[pl.ds(2 * LINE + 2 * n + g, ROWS, stride=GROUPS), :] = hidden[
                    :, 128 * g : 128 * (g + 1)
                ]
        puts.append(copies.start(pv, outs._proj))
        puts.append(copies.start(map2, outs._map2))
        depthwise(map2, wide2, work, 2, False)

        def collect_second(p, g, rows, cols):
            sv[rows, cols] = map_to_rows(work, p, g).astype(BF)

        tiles(collect_second)
        puts.append(copies.by_core(core, sv, outs._send, outs._keep))
        for n in range(4):
            cols = pl.ds(256 * n, 256)
            branch = dot(sv[...], w2[:, cols], ((1,), (0,)))
            x_out[:, cols] = (xv[:, cols].astype(F32) + branch).astype(BF)
        for put in puts:
            put.wait()


def forward(moment, images, came, k1, k2, p1, p2, after):
    ins = dict(k1=k1, k2=k2, came=came, _after=after)
    ins.update(dict(p1=p1, p2=p2) if moment > 0 else dict(_p1=p1, _p2=p2))
    outs = dict(
        x=rows_type(),
        _map1=map_type(MAP1),
        _map2=map_type(MAP2),
        _proj=rows_type(),
        _keep=rows_type(),
        _send=rows_type(),
    )
    if moment < MICRO:
        ins.update(_images=images)
    if moment > 0:
        outs.update(_x=rows_type())
    return call(
        functools.partial(forward_body, moment),
        ins,
        outs,
        [
            rows_scratch(),
            map_scratch(72),
            map_scratch(72),
            map_scratch(MAP1),
            map_scratch(MAP2),
            map_scratch(FLAT),
            rows_scratch(),
            rows_scratch(),
            rows_scratch(),
            pltpu.SemaphoreType.DMA((10,)),
            *([rows_scratch(C), rows_scratch(C)] if moment == 0 else []),
        ],
        8 if moment > 0 else 14,
        f"fwd{moment}",
        4 * ROWS * C * C,
        8 * MIB,
    )


def backward_pairs(moment):
    found = []
    for section in range(SECTIONS):
        micro = moment - (2 * SECTIONS - 2) + section
        if 0 <= micro < MICRO:
            found.append((section, micro, micro + section))
    return found


def is_active(section, pairs):
    return functools.reduce(lambda a, b: a | b, [section == s for s, _, _ in pairs])


def backward_body(moment, ins, outs, scratch):
    gs, xs, ps, wide1, wide2, map1, map2, work, hv, sems = scratch
    pairs = backward_pairs(moment)
    section = lax.axis_index(SECTION)
    core = this_core()

    @pl.when(is_active(section, pairs))
    def _():
        copies = Copies(sems)
        g_out = outs.g
        top = [micro for s, micro, _ in pairs if s == SECTIONS - 1]
        if top:
            get_g = pltpu.make_async_copy(ins._cotangent.at[top[0]], gs, copies.next())
            pl.when(section == SECTIONS - 1)(get_g.start)
        parts = [pl.ds(QUARTER * n, QUARTER) for n in range(4)]
        get_p = copies.by_section(section, {s: ins._proj[when] for s, _, when in pairs}, ps)
        get_x = copies.by_section(section, {s: ins._x[when] for s, _, when in pairs if s > 0}, xs)
        widen_kernel(ins.k1, wide1)
        widen_kernel(ins.k2, wide2)
        clear_edges(map1, 1)
        clear_edges(map2, 2)
        came = {s: ins.came[s % 2] for s, _, _ in pairs if s < SECTIONS - 1}
        if top:
            pl.when(section == SECTIONS - 1)(get_g.wait)
            for s, ref in came.items():

                @pl.when(section == s)
                def _(ref=ref):
                    gs[...] = ref[...]

        gv = gs if top else pick(section, gs, came)
        for n in range(4):
            part = dot(gv[...], ins.p2[parts[n], :], ((1,), (1,)))
            part = part.astype(BF).astype(F32)
            for g in range(2):
                map2[pl.ds(2 * LINE + 2 * n + g, ROWS, stride=GROUPS), :] = part[
                    :, 128 * g : 128 * (g + 1)
                ]
        puts = [copies.by_core(core, gv, outs._send, outs._keep)]
        puts.append(copies.start(map2, outs._map2))
        depthwise(map2, wide2, work, 2, True)
        get_p.wait()

        def collect_hidden(p, g, rows, cols):
            hv[rows, cols] = (map_to_rows(work, p, g) * slope(ps[rows, cols].astype(F32))).astype(BF)

        tiles(collect_hidden)
        puts.append(copies.by_core(core, hv, outs._keep, outs._send))
        for n in range(4):
            part = dot(hv[...], ins.p1[parts[n], :], ((1,), (1,)))
            part = part.astype(BF).astype(F32)
            for g in range(2):
                map1[pl.ds(LINE + 2 * n + g, ROWS, stride=GROUPS), :] = part[
                    :, 128 * g : 128 * (g + 1)
                ]
        puts.append(copies.start(map1, outs._map1))

        @pl.when(section != 0)
        def _():
            get_x.wait()
            depthwise(map1, wide1, work, 1, True)

            def collect(p, g, rows, cols):
                back = map_to_rows(work, p, g) * slope(xs[rows, cols].astype(F32))
                g_out[rows, cols] = (gv[rows, cols].astype(F32) + back).astype(BF)

            tiles(collect)

        for put in puts:
            put.wait()


def backward(moment, cotangent, came, xs, projs, k1, k2, p1, p2, after):
    ins = dict(k1=k1, k2=k2, p1=p1, p2=p2, _x={}, _proj={}, _after=after, came=came)
    for s, micro, when in backward_pairs(moment):
        if s == SECTIONS - 1:
            ins.update(_cotangent=cotangent)
        if s > 0:
            ins["_x"][when] = xs[when]
        ins["_proj"][when] = projs[when]
    return call(
        functools.partial(backward_body, moment),
        ins,
        dict(
            g=rows_type(),
            _map2=map_type(MAP2),
            _map1=map_type(MAP1),
            _keep=rows_type(),
            _send=rows_type(),
        ),
        [
            rows_scratch(),
            rows_scratch(),
            rows_scratch(),
            map_scratch(72),
            map_scratch(72),
            map_scratch(MAP1),
            map_scratch(MAP2),
            map_scratch(FLAT),
            rows_scratch(),
            pltpu.SemaphoreType.DMA((12,)),
        ],
        8,
        f"bwd{moment}",
        4 * ROWS * C * C,
        8 * MIB,
    )


def taps_body(moment, ins, outs, scratch):
    s1, s2, g1, g2, sems = scratch
    out = outs.sums
    pairs = backward_pairs(moment)
    section = lax.axis_index(SECTION)
    active = is_active(section, pairs)

    @pl.when(active)
    def _():
        copies = Copies(sems)
        get = [copies.by_section(section, {s: ins._s2[when] for s, _, when in pairs}, s2)]
        get.append(copies.start(ins._g2, g2))
        later = [copies.by_section(section, {s: ins._s1[when] for s, _, when in pairs}, s1)]
        later.append(copies.start(ins._g1, g1))
        for start, field, grad, dilation, waits in ((9, s2, g2, 2, get), (0, s1, g1, 1, later)):
            for copy in waits:
                copy.wait()
            found = kernel_grad(field, grad, dilation)
            for t in range(9):
                rows = pl.ds(8 * (start + t), 8)
                out[rows, :] = found[t] + (ins.sums[rows, :] if moment > SECTIONS - 1 else 0.0)

    @pl.when(jnp.logical_not(active))
    def _():
        out[...] = ins.sums[...] if moment > SECTIONS - 1 else jnp.zeros_like(out)


def taps(moment, sums, maps1, maps2, g1, g2, after):
    ins = dict(_g1=g1, _g2=g2, _s1={}, _s2={}, _after=after)
    if sums is not None:
        ins.update(sums=sums)
    for s, micro, when in backward_pairs(moment):
        ins["_s1"][when] = maps1[when]
        ins["_s2"][when] = maps2[when]
    return call(
        functools.partial(taps_body, moment),
        ins,
        dict(sums=map_type(18 * GROUPS)),
        [
            map_scratch(MAP1),
            map_scratch(MAP2),
            map_scratch(MAP1),
            map_scratch(MAP2),
            pltpu.SemaphoreType.DMA((4,)),
        ],
        6,
        f"taps{moment}",
        40 * ROWS * C,
        3 * MIB,
    ).sums


QUARTER = C // 4
HALF = QUARTER // 2
SMALL = 16


def places():
    replica = lax.axis_index(REPLICA)
    core = lax.rem(replica, 2)
    x = lax.rem(lax.div(replica, 2), 4)
    y = lax.div(replica, 8)
    return core, jnp.where(core == 0, x, y), jnp.where(core == 0, y, x)


def gather_operands(operands, micros):
    ahead = [m + s for m in micros for s in range(SECTIONS)]
    back = [m + 2 * SECTIONS - 2 - s for m in micros for s in range(SECTIONS)]
    left = [{t: value[t] for t in ahead} for value in operands[:2]]
    right = [{t: value[t] for t in back} for value in operands[2:]]
    return dict(_lefts=left, _rights=right)


def stack_operands(ins, micros, left, right, sems):
    section = lax.axis_index(SECTION)
    for s in range(SECTIONS):

        @pl.when(section == s)
        def _(s=s):
            for n, m in enumerate(micros):
                ahead, back = m + s, m + 2 * SECTIONS - 2 - s
                for h in range(2):
                    k = 2 * n + h
                    rows = pl.ds(k * ROWS, ROWS)
                    a, b = ins._lefts[h][ahead], ins._rights[h][back]
                    pltpu.make_async_copy(a, left.at[rows, :], sems.at[2 * k]).start()
                    pltpu.make_async_copy(b, right.at[rows, :], sems.at[2 * k + 1]).start()

    for k in range(2 * len(micros)):
        rows = pl.ds(k * ROWS, ROWS)
        pltpu.make_async_copy(left.at[rows, :], left.at[rows, :], sems.at[2 * k]).wait()
        pltpu.make_async_copy(right.at[rows, :], right.at[rows, :], sems.at[2 * k + 1]).wait()


def early_body(micros, ins, outs, scratch):
    left, right, sems = scratch
    out = outs.early
    stack_operands(ins, micros, left, right, sems)

    def part(n, carry):
        start = pl.multiple_of(n * QUARTER, QUARTER)
        out[pl.ds(start, QUARTER), :] = dot(left[:, pl.ds(start, QUARTER)], right[...], ((0,), (0,)))
        return carry

    lax.fori_loop(0, 4, part, 0)


def early_weights(operands):
    micros = tuple(range(MICRO - 1))
    size = 2 * len(micros) * ROWS
    return call(
        functools.partial(early_body, micros),
        gather_operands(operands, micros),
        dict(early=jax.ShapeDtypeStruct((C, C), F32)),
        [rows_scratch(size), rows_scratch(size), pltpu.SemaphoreType.DMA((4 * len(micros),))],
        12,
        "early_weights",
        2 * size * C * C,
        8 * MIB,
    ).early


def part_of(early, left, right, number):
    start = pl.multiple_of(lax.rem(number, 4) * QUARTER, QUARTER)
    added = dot(left[:, pl.ds(start, QUARTER)], right[...], ((0,), (0,)))
    return early[pl.ds(start, QUARTER), :] + added


def far_body(ins, outs, scratch):
    (sems,) = scratch
    left, right = outs.left, outs.right
    stack_operands(ins, (MICRO - 1,), left, right, sems)
    _, mine, _ = places()
    whole = part_of(ins.early, left, right, mine + 2).astype(BF)
    outs.up[...] = whole[:HALF]
    outs.low[...] = whole[HALF:]


def far_part(operands, early):
    size = 2 * ROWS
    return call(
        far_body,
        dict(early=early, **gather_operands(operands, (MICRO - 1,))),
        dict(
            up=rows_type(HALF),
            low=rows_type(HALF),
            left=rows_type(size),
            right=rows_type(size),
        ),
        [pltpu.SemaphoreType.DMA((4,))],
        8,
        "far_part",
        2 * size * C * QUARTER,
        3 * MIB,
    )


def tail_body(ins, outs, scratch):
    small, wide = scratch
    both = ins.sums[...] + ins.other[...]
    small[...] = jnp.where(this_core() == 0, both[:72], both[72:])
    wide[...] = jnp.zeros((SMALL, C), F32)
    for g in range(GROUPS):
        wide[pl.ds(0, 9), 128 * g : 128 * (g + 1)] = small[pl.ds(g, 9, stride=GROUPS), :]
    outs.tail[...] = wide[...].astype(BF)


def tail_part(sums, other):
    return call(
        tail_body,
        dict(sums=sums, other=other),
        dict(tail=rows_type(SMALL)),
        [map_scratch(72), pltpu.VMEM((SMALL, C), F32)],
        2,
        "tail",
        0,
        MIB,
    ).tail


def near_body(ins, outs, scratch):
    _, mine, _ = places()
    after = part_of(ins.early, ins.left, ins.right, mine + 1)
    outs.after_up[...] = after[:HALF]
    outs.after_low[...] = after[HALF:].astype(BF)
    before = part_of(ins.early, ins.left, ins.right, mine + 3)
    outs.before_up[...] = before[:HALF].astype(BF)
    outs.before_low[...] = before[HALF:]
    outs.own[...] = part_of(ins.early, ins.left, ins.right, mine)


def wide_type(n):
    return jax.ShapeDtypeStruct((n, C), F32)


def near_parts(early, left, right):
    return call(
        near_body,
        dict(early=early, left=left, right=right),
        dict(
            after_up=wide_type(HALF),
            after_low=rows_type(HALF),
            before_up=rows_type(HALF),
            before_low=wide_type(HALF),
            own=wide_type(QUARTER),
        ),
        [],
        8,
        "near_parts",
        2 * 2 * ROWS * C * QUARTER * 3,
        8 * MIB,
    )


def relay_body(ins, outs, scratch):
    outs.after[...] = (ins.after[...] + ins.up[...].astype(F32)).astype(BF)
    outs.before[...] = (ins.before[...] + ins.low[...].astype(F32)).astype(BF)


def relay(after, before, up, low, waits):
    return call(
        relay_body,
        dict(after=after, before=before, up=up, low=low, _after=waits),
        dict(after=rows_type(HALF), before=rows_type(HALF)),
        [],
        4,
        "relay",
        0,
        4 * MIB,
    )


def mark_body(ins, outs, scratch):
    outs.mark[...] = jnp.zeros_like(outs.mark)


def after_both_cores(values):
    mark = call(mark_body, dict(_after=values), dict(mark=map_type(8)), [], 1, "mark", 0, 4096).mark
    return to_core(mark)


def ring_sum(a, b, c, d):
    a, b, c, d = (value.astype(F32) for value in (a, b, c, d))
    return (a + b) + (c + d)


def first_sum_body(ins, outs, scratch):
    up, low = [a.astype(F32) + b.astype(F32) for a, b in ((ins.ups[0][...], ins.ups[1][...]), (ins.lows[0][...], ins.lows[1][...]))]
    outs.up[pl.ds(0, HALF), :] = (ins.own[:HALF] + up).astype(BF)
    outs.up[pl.ds(HALF, SMALL), :] = ins.tail[...]
    outs.low[...] = (ins.own[HALF:] + low).astype(BF)


def first_sum(own, ups, lows, tail, waits):
    found = call(
        first_sum_body,
        dict(own=own, ups=ups, lows=lows, tail=tail, _after=waits),
        dict(up=rows_type(HALF + SMALL), low=rows_type(HALF)),
        [],
        4,
        "first_sum",
        0,
        4 * MIB,
    )
    return found.up, found.low


def pair_sum_body(ins, outs, scratch):
    outs.up[...] = (ins.up[...].astype(F32) + ins.up_came[...].astype(F32)).astype(BF)
    outs.low[...] = (ins.low[...].astype(F32) + ins.low_came[...].astype(F32)).astype(BF)


def pair_sum(up, low, up_came, low_came, waits):
    found = call(
        pair_sum_body,
        dict(up=up, low=low, up_came=up_came, low_came=low_came, _after=waits),
        dict(up=rows_type(HALF + SMALL), low=rows_type(HALF)),
        [],
        3,
        "pair_sum",
        0,
        2 * MIB,
    )
    return found.up, found.low


def other_a(place):
    return place + 1 - 2 * lax.rem(place, 2)


def other_b(place):
    return 3 - place


def convert(outs, blocks, wide, sems):
    core, mine, its = places()
    waits = []
    for n, (part, low, own, by_a, by_b) in enumerate(blocks):
        place = mine if own else its
        place = other_a(place) if by_a else place
        place = other_b(place) if by_b else place
        slot, sem = wide.at[n], sems.at[n]
        slot[...] = part[pl.ds(0, HALF), :].astype(F32)
        rows = pl.ds(pl.multiple_of(place * QUARTER + low * HALF, HALF), HALF)

        @pl.when(core == (0 if own else 1))
        def _(slot=slot, rows=rows, sem=sem):
            pltpu.make_async_copy(slot, outs._point1.at[0, rows, :], sem).start()

        @pl.when(core == (1 if own else 0))
        def _(slot=slot, rows=rows, sem=sem):
            pltpu.make_async_copy(slot, outs._point2.at[0, rows, :], sem).start()

        waits.append(pltpu.make_async_copy(slot, slot, sem))
    for copy in waits:
        copy.wait()


POINT = jax.ShapeDtypeStruct((1, C, C), F32)


def write_body(kinds, with_tails, ins, outs, scratch):
    if with_tails:
        own, its = [
            ring_sum(*[ins.tails[n][k][pl.ds(HALF, SMALL), :] for k in range(4)])[:9] for n in range(2)
        ]
        core = this_core()
        outs.small1[:, 0, :] = jnp.where(core == 0, own, its)
        outs.small2[:, 0, :] = jnp.where(core == 0, its, own)
    convert(outs, [(ins.parts[n], *kind) for n, kind in enumerate(kinds)], *scratch)


def write(blocks, begun, tails):
    parts = [block[0] for block in blocks]
    ins, outs = dict(parts=parts), dict(_point1=POINT, _point2=POINT)
    aliases = None
    if begun is not None:
        ins.update(_was1=begun._point1, _was2=begun._point2)
        aliases = dict(_was1="_point1", _was2="_point2")
    if tails:
        small = jax.ShapeDtypeStruct((9, 1, C), F32)
        ins.update(tails=tails)
        outs.update(small1=small, small2=small)
    return call(
        functools.partial(write_body, [block[1:] for block in blocks], bool(tails)),
        ins,
        outs,
        [pltpu.VMEM((len(blocks), HALF, C), F32), pltpu.SemaphoreType.DMA((len(blocks),))],
        10,
        "write",
        100 * MIB,
        len(blocks) * HALF * C * 6,
        aliases,
    )


def to_replica(value, target):
    return lax.ppermute(value, REPLICA, [(r, target(r)) for r in range(32)])


def to_core(value):
    return to_replica(value, lambda r: r ^ 1)


def along_x(r, d):
    return (r // 8) * 8 + ((r // 2 + d) % 4) * 2 + r % 2


def along_y(r, d):
    return ((r // 8 + d) % 4) * 8 + r % 8


def along_first(value, d):
    return to_replica(value, lambda r: along_x(r, d) if r % 2 == 0 else along_y(r, d))


def pair_a(value, first):
    return to_pair(value, first, lambda place: place ^ 1)


def pair_b(value, first):
    return to_pair(value, first, lambda place: 3 - place)


def to_pair(value, first, partner):
    def target(r):
        x, y, core = (r // 2) % 4, r // 8, r % 2
        if (core == 0) == first:
            x = partner(x)
        else:
            y = partner(y)
        return y * 8 + x * 2 + core

    return to_replica(value, target)


def to_neighbours(value, pairs):
    came = {}
    for source, target in pairs:
        near = min(source, target) % 2 == 0
        if target % 2 not in came:
            swap = [(s, s ^ 1 if near else 3 - s) for s in range(SECTIONS)]
            came[target % 2] = lax.ppermute(value, SECTION, swap)
    return came


def per_device(images, cotangent, depth_first, point_first, depth_second, point_second):
    images = images.reshape(MICRO, ROWS, C)
    cotangent = cotangent.reshape(MICRO, ROWS, C)
    weights = (depth_first[0], depth_second[0], point_first[0], point_second[0])
    xs, projs, maps1, maps2 = {}, {}, {}, {}
    operands = ({}, {}, {}, {})
    grads1, grads2 = {}, {}
    came, returned = {}, {}
    sums = early = None
    last = 3 * SECTIONS - 3
    full = MICRO + SECTIONS - 2
    for moment in range(last + 1):
        if moment <= full:
            after = [operands[1][moment - 2]] if 1 < moment < MICRO else []
            found = forward(moment, images, came, *weights, after)
            maps1[moment], maps2[moment] = found._map1, found._map2
            projs[moment] = found._proj
            if moment > 0:
                xs[moment] = found._x
            operands[0][moment] = found._keep
            operands[1][moment] = to_core(found._send)
            going = [(s, s + 1) for s in forward_sections(moment) if s < SECTIONS - 1]
            came = to_neighbours(found.x, sorted(going, reverse=True))
        if moment >= SECTIONS - 1:
            after = [] if sums is None else [sums]
            after += [] if early is None else [early]
            if moment == full + 1:
                after += [operands[1][past] for past in range(MICRO - 2, full + 1)]
            if moment == full + 2:
                after += [operands[3][past] for past in range(SECTIONS - 1, full + 1)]
            found = backward(moment, cotangent, returned, xs, projs, *weights, after)
            grads2[moment], grads1[moment] = found._map2, found._map1
            operands[2][moment] = found._keep
            operands[3][moment] = to_core(found._send)
            going = [(s, s - 1) for s, _, _ in backward_pairs(moment) if s > 0]
            returned = to_neighbours(found.g, sorted(going, reverse=True))
        if full <= moment < last:
            for past in range(SECTIONS - 1, moment + 1) if moment == full else [moment]:
                sums = taps(past, sums, maps1, maps2, grads1[past], grads2[past], [grads1[moment]])
        if moment == last - 1:
            early = early_weights(operands)
    far = far_part(operands, early)
    sums = taps(last, sums, maps1, maps2, grads1[last], grads2[last], [far.left])
    up, low = along_first(far.up, 1), along_first(far.low, -1)
    near = near_parts(early, far.left, far.right)
    near_low, near_up = along_first(near.after_low, 1), along_first(near.before_up, -1)
    sent = relay(near.after_up, near.before_low, up, low, [sums])
    tail = tail_part(sums, to_core(sums))
    up, low = along_first(sent.after, 1), along_first(sent.before, -1)
    both = after_both_cores([up, low])
    up, low = first_sum(near.own, [up, near_up], [near_low, low], tail, [both])
    up, low = pair_sum(up, low, pair_a(up, False), pair_b(low, False), [])
    up_came, low_came = pair_b(up, False), pair_a(low, False)
    both = after_both_cores([up_came, low_came])
    up, low = pair_sum(up, low, up_came, low_came, [both])
    up_a, low_b = pair_a(up, True), pair_b(low, True)
    up_b, low_a = pair_b(up, True), pair_a(low, True)
    up_ab, low_ab = pair_b(up_a, True), pair_a(low_b, True)
    own = [[up, up_a, up_ab, up_b], [low, low_a, low_ab, low_b]]
    its = [[to_core(value) for value in values] for values in own]
    came = ((0, 0), (1, 0), (1, 1), (0, 1))
    blocks = [
        (values[low][n], low, values is own, *came[n])
        for values in (own, its)
        for n in (0, 1, 3, 2)
        for low in (0, 1)
    ]
    late = [block for block in blocks if block[3:] == (1, 1)]
    begun = write([block for block in blocks if block[3:] != (1, 1)], None, None)
    done = write(late, begun, [own[0], its[0]])
    small1, small2 = jnp.swapaxes(done.small1, 0, 1), jnp.swapaxes(done.small2, 0, 1)
    return small1, done._point1, small2, done._point2


def solution(mesh):
    sharded = P(None, REPLICA, None, None, None)
    by_section = P(SECTION, None, None)
    return jax.shard_map(
        per_device,
        mesh=mesh,
        in_specs=(sharded, sharded) + (by_section,) * 4,
        out_specs=(by_section,) * 4,
        check_vma=False,
    )
```

```python
import functools
from types import SimpleNamespace

import jax
import jax.numpy as jnp
from jax import lax
from jax.experimental import pallas as pl
from jax.experimental.pallas import tpu as pltpu
from jax.sharding import PartitionSpec as P

BF = jnp.bfloat16
F32 = jnp.float32
SIDE = 12
ROWS = SIDE * SIDE
C = 1024
GROUPS = C // 128
LINE = SIDE * GROUPS
MICRO = 4
SECTIONS = 4
MAP1 = (SIDE + 2) * LINE
MAP2 = (SIDE + 4) * LINE
FLAT = SIDE * LINE
MIB = 1024 * 1024
SECTION = "section"
REPLICA = "replica"

ANY = pl.BlockSpec(memory_space=pl.ANY)
VM = pl.BlockSpec(memory_space=pltpu.VMEM)


def sigmoid(v):
    return 0.5 * jnp.tanh(0.5 * v) + 0.5


def slope(v):
    s = sigmoid(v)
    return s * (1.0 + v * (1.0 - s))


def widen_kernel(k_ref, wide):
    for g in range(GROUPS):
        wide[pl.ds(g, 9, stride=GROUPS), :] = k_ref[:, 128 * g : 128 * (g + 1)].astype(F32)


def clear_edges(field, dilation):
    size = dilation * LINE
    zero = jnp.zeros((size, 128), F32)
    field[pl.ds(0, size), :] = zero
    field[pl.ds(FLAT + size, size), :] = zero


def depthwise(field, wide, out, dilation, flip):
    taps = [wide[pl.ds(8 * (8 - t if flip else t), 8), :] for t in range(9)]

    def line(i, carry):
        seen = {}

        def at(p, j):
            if (p, j) not in seen:
                start = pl.multiple_of((i + p * dilation) * LINE + j * GROUPS, 8)
                seen[p, j] = field[pl.ds(start, 8), :]
            return seen[p, j]

        for j in range(SIDE):
            total = None
            for t in range(9):
                p, q = divmod(t, 3)
                col = j + (q - 1) * dilation
                if 0 <= col < SIDE:
                    term = taps[t] * at(p, col)
                    total = term if total is None else total + term
            out[pl.ds(pl.multiple_of(i * LINE + j * GROUPS, 8), 8), :] = total
        return carry

    lax.fori_loop(0, SIDE, line, 0)


def kernel_grad(field, grad, dilation):
    def line(i, sums):
        sums = list(sums)
        seen = {}

        def at(p, j):
            if (p, j) not in seen:
                start = pl.multiple_of((i + p * dilation) * LINE + j * GROUPS, 8)
                seen[p, j] = field[pl.ds(start, 8), :]
            return seen[p, j]

        for j in range(SIDE):
            here = grad[pl.ds(pl.multiple_of((i + dilation) * LINE + j * GROUPS, 8), 8), :]
            for t in range(9):
                p, q = divmod(t, 3)
                col = j + (q - 1) * dilation
                if 0 <= col < SIDE:
                    sums[t] = sums[t] + here * at(p, col)
        return tuple(sums)

    return lax.fori_loop(0, SIDE, line, tuple(jnp.zeros((8, 128), F32) for _ in range(9)))


def rows_to_map(field, base, p, g, value):
    field[pl.ds(base + 16 * p * GROUPS + g, 16, stride=GROUPS), :] = value


def map_to_rows(field, p, g):
    return field[pl.ds(16 * p * GROUPS + g, 16, stride=GROUPS), :]


def tiles(body):
    def step(p, carry):
        for g in range(GROUPS):
            body(p, g, pl.ds(pl.multiple_of(16 * p, 16), 16), pl.ds(128 * g, 128))
        return carry

    lax.fori_loop(0, ROWS // 16, step, 0)


def dot(a, b, dims):
    return lax.dot_general(a, b, (dims, ((), ())), preferred_element_type=F32)


def rows_type(n=ROWS):
    return jax.ShapeDtypeStruct((n, C), BF)


def map_type(n):
    return jax.ShapeDtypeStruct((n, 128), F32)


def call(body, ins, outs, scratch, limit, name, flops, size, aliases=None):
    flat, tree = jax.tree.flatten(ins)
    out_flat, out_tree = jax.tree.flatten(outs)

    def kernel(*refs):
        first, last = len(flat), len(flat) + len(out_flat)
        given = SimpleNamespace(**jax.tree.unflatten(tree, refs[:first]))
        made = SimpleNamespace(**jax.tree.unflatten(out_tree, refs[first:last]))
        body(given, made, refs[last:])

    def names(arrays):
        return jax.tree.leaves({n: jax.tree.map(lambda _: n, value) for n, value in arrays.items()})

    def specs(arrays):
        return [ANY if n.startswith("_") else VM for n in names(arrays)]

    found = pl.pallas_call(
        kernel,
        out_shape=out_flat,
        in_specs=specs(ins),
        out_specs=specs(outs),
        scratch_shapes=scratch,
        input_output_aliases={
            names(ins).index(a): names(outs).index(b) for a, b in (aliases or {}).items()
        },
        compiler_params=pltpu.CompilerParams(vmem_limit_bytes=limit * MIB),
        cost_estimate=pl.CostEstimate(flops=flops, bytes_accessed=size, transcendentals=0),
        name=name,
    )(*flat)
    return SimpleNamespace(**jax.tree.unflatten(out_tree, found))


class Copies:
    def __init__(self, sems):
        self.sems = sems
        self.count = 0

    def next(self):
        self.count += 1
        return self.sems.at[self.count - 1]

    def start(self, source, target):
        copy = pltpu.make_async_copy(source, target, self.next())
        copy.start()
        return copy

    def by_section(self, section, choices, target):
        sem = self.next()
        for s, source in choices.items():

            @pl.when(section == s)
            def _(source=source):
                pltpu.make_async_copy(source, target, sem).start()

        return pltpu.make_async_copy(target, target, sem)

    def by_core(self, core, value, on_zero, on_one):
        sem = self.next()

        @pl.when(core == 0)
        def _():
            pltpu.make_async_copy(value, on_zero, sem).start()

        @pl.when(core == 1)
        def _():
            pltpu.make_async_copy(value, on_one, sem).start()

        return pltpu.make_async_copy(value, value, sem)


def this_core():
    return lax.rem(lax.axis_index(REPLICA), 2)


def rows_scratch(n=ROWS):
    return pltpu.VMEM((n, C), BF)


def map_scratch(n):
    return pltpu.VMEM((n, 128), F32)


def pick(section, target, choices):
    if len(choices) == 1:
        return next(iter(choices.values()))
    for s, ref in choices.items():

        @pl.when(section == s)
        def _(ref=ref):
            target[...] = ref[...]

    return target


def forward_sections(moment):
    return [s for s in range(SECTIONS) if 0 <= moment - s < MICRO]


def forward_body(moment, ins, outs, scratch):
    xs, wide1, wide2, map1, map2, work, fv, sv, pv, sems, *own = scratch
    section = lax.axis_index(SECTION)
    core = this_core()
    slot = moment - section

    @pl.when((slot >= 0) & (slot < MICRO))
    def _():
        copies = Copies(sems)
        x_out = outs.x
        if moment < MICRO:
            get_x = pltpu.make_async_copy(ins._images.at[moment], xs, copies.next())
            pl.when(section == 0)(get_x.start)
        puts = []
        if own:
            w1, w2 = own
            gets = [copies.start(ins._p1, w1), copies.start(ins._p2, w2)]
        else:
            w1, w2 = ins.p1, ins.p2
        widen_kernel(ins.k1, wide1)
        widen_kernel(ins.k2, wide2)
        clear_edges(map1, 1)
        clear_edges(map2, 2)
        if moment < MICRO:
            pl.when(section == 0)(get_x.wait)
        came = {s: ins.came[s % 2] for s in forward_sections(moment) if s > 0}
        if moment < MICRO and moment > 0:
            came[0] = xs
            for s, ref in came.items():
                if s > 0:

                    @pl.when(section == s)
                    def _(ref=ref):
                        xs[...] = ref[...]

        xv = xs if moment < MICRO else pick(section, xs, came)
        if moment > 0:
            puts.append(copies.start(xv, outs._x))

        def enter(p, g, rows, cols):
            v = xv[rows, cols].astype(F32)
            rows_to_map(map1, LINE, p, g, v * sigmoid(v))

        tiles(enter)
        depthwise(map1, wide1, work, 1, False)

        def collect_first(p, g, rows, cols):
            fv[rows, cols] = map_to_rows(work, p, g).astype(BF)

        tiles(collect_first)
        if own:
            for get in gets:
                get.wait()
        puts.append(copies.start(map1, outs._map1))
        puts.append(copies.by_core(core, fv, outs._keep, outs._send))
        for n in range(4):
            cols = pl.ds(256 * n, 256)
            pre = dot(fv[...], w1[:, cols], ((1,), (0,)))
            pv[:, cols] = pre.astype(BF)
            hidden = (pre * sigmoid(pre)).astype(BF).astype(F32)
            for g in range(2):
                map2[pl.ds(2 * LINE + 2 * n + g, ROWS, stride=GROUPS), :] = hidden[
                    :, 128 * g : 128 * (g + 1)
                ]
        puts.append(copies.start(pv, outs._proj))
        puts.append(copies.start(map2, outs._map2))
        depthwise(map2, wide2, work, 2, False)

        def collect_second(p, g, rows, cols):
            sv[rows, cols] = map_to_rows(work, p, g).astype(BF)

        tiles(collect_second)
        puts.append(copies.by_core(core, sv, outs._send, outs._keep))

        @pl.when(section != SECTIONS - 1)
        def _():
            for n in range(4):
                cols = pl.ds(256 * n, 256)
                branch = dot(sv[...], w2[:, cols], ((1,), (0,)))
                x_out[:, cols] = (xv[:, cols].astype(F32) + branch).astype(BF)

        for put in puts:
            put.wait()


def forward(moment, images, came, k1, k2, p1, p2, after):
    ins = dict(k1=k1, k2=k2, came=came, _after=after)
    ins.update(dict(p1=p1, p2=p2) if moment > 0 else dict(_p1=p1, _p2=p2))
    outs = dict(
        x=rows_type(),
        _map1=map_type(MAP1),
        _map2=map_type(MAP2),
        _proj=rows_type(),
        _keep=rows_type(),
        _send=rows_type(),
    )
    if moment < MICRO:
        ins.update(_images=images)
    if moment > 0:
        outs.update(_x=rows_type())
    return call(
        functools.partial(forward_body, moment),
        ins,
        outs,
        [
            rows_scratch(),
            map_scratch(72),
            map_scratch(72),
            map_scratch(MAP1),
            map_scratch(MAP2),
            map_scratch(FLAT),
            rows_scratch(),
            rows_scratch(),
            rows_scratch(),
            pltpu.SemaphoreType.DMA((10,)),
            *([rows_scratch(C), rows_scratch(C)] if moment == 0 else []),
        ],
        8 if moment > 0 else 14,
        f"fwd{moment}",
        4 * ROWS * C * C,
        8 * MIB,
    )


def turn_body(ins, outs, scratch):
    for out, value in ((outs.p1, ins.p1), (outs.p2, ins.p2)):
        for n in range(4):
            for m in range(4):
                rows, cols = pl.ds(256 * n, 256), pl.ds(256 * m, 256)
                out[cols, rows] = value[rows, cols].T


def turned(p1, p2, after):
    square = rows_type(C)
    found = call(
        turn_body,
        dict(p1=p1, p2=p2, _after=after),
        dict(p1=square, p2=square),
        [],
        8,
        "turn",
        100 * MIB,
        8 * MIB,
    )
    return found.p1, found.p2


def backward_pairs(moment):
    found = []
    for section in range(SECTIONS):
        micro = moment - (2 * SECTIONS - 2) + section
        if 0 <= micro < MICRO:
            found.append((section, micro, micro + section))
    return found


def is_active(section, pairs):
    return functools.reduce(lambda a, b: a | b, [section == s for s, _, _ in pairs])


def backward_body(moment, ins, outs, scratch):
    gs, xs, ps, wide1, wide2, map1, map2, work, hv, sems = scratch
    pairs = backward_pairs(moment)
    section = lax.axis_index(SECTION)
    core = this_core()

    @pl.when(is_active(section, pairs))
    def _():
        copies = Copies(sems)
        g_out = outs.g
        top = [micro for s, micro, _ in pairs if s == SECTIONS - 1]
        if top:
            get_g = pltpu.make_async_copy(ins._cotangent.at[top[0]], gs, copies.next())
            pl.when(section == SECTIONS - 1)(get_g.start)
        parts = [pl.ds(QUARTER * n, QUARTER) for n in range(4)]
        get_p = copies.by_section(section, {s: ins._proj[when] for s, _, when in pairs}, ps)
        get_x = copies.by_section(section, {s: ins._x[when] for s, _, when in pairs if s > 0}, xs)
        widen_kernel(ins.k1, wide1)
        widen_kernel(ins.k2, wide2)
        clear_edges(map1, 1)
        clear_edges(map2, 2)
        came = {s: ins.came[s % 2] for s, _, _ in pairs if s < SECTIONS - 1}
        if top:
            pl.when(section == SECTIONS - 1)(get_g.wait)
            for s, ref in came.items():

                @pl.when(section == s)
                def _(ref=ref):
                    gs[...] = ref[...]

        gv = gs if top else pick(section, gs, came)
        for n in range(4):
            part = dot(gv[...], ins.p2[:, parts[n]], ((1,), (0,)))
            part = part.astype(BF).astype(F32)
            for g in range(2):
                map2[pl.ds(2 * LINE + 2 * n + g, ROWS, stride=GROUPS), :] = part[
                    :, 128 * g : 128 * (g + 1)
                ]
        puts = [copies.by_core(core, gv, outs._send, outs._keep)]
        puts.append(copies.start(map2, outs._map2))
        depthwise(map2, wide2, work, 2, True)
        get_p.wait()

        def collect_hidden(p, g, rows, cols):
            hv[rows, cols] = (map_to_rows(work, p, g) * slope(ps[rows, cols].astype(F32))).astype(BF)

        tiles(collect_hidden)
        puts.append(copies.by_core(core, hv, outs._keep, outs._send))
        for n in range(4):
            part = dot(hv[...], ins.p1[:, parts[n]], ((1,), (0,)))
            part = part.astype(BF).astype(F32)
            for g in range(2):
                map1[pl.ds(LINE + 2 * n + g, ROWS, stride=GROUPS), :] = part[
                    :, 128 * g : 128 * (g + 1)
                ]
        puts.append(copies.start(map1, outs._map1))

        @pl.when(section != 0)
        def _():
            get_x.wait()
            depthwise(map1, wide1, work, 1, True)

            def collect(p, g, rows, cols):
                back = map_to_rows(work, p, g) * slope(xs[rows, cols].astype(F32))
                g_out[rows, cols] = (gv[rows, cols].astype(F32) + back).astype(BF)

            tiles(collect)

        for put in puts:
            put.wait()


def backward(moment, cotangent, came, xs, projs, k1, k2, p1, p2, after):
    ins = dict(k1=k1, k2=k2, p1=p1, p2=p2, _x={}, _proj={}, _after=after, came=came)
    for s, micro, when in backward_pairs(moment):
        if s == SECTIONS - 1:
            ins.update(_cotangent=cotangent)
        if s > 0:
            ins["_x"][when] = xs[when]
        ins["_proj"][when] = projs[when]
    return call(
        functools.partial(backward_body, moment),
        ins,
        dict(
            g=rows_type(),
            _map2=map_type(MAP2),
            _map1=map_type(MAP1),
            _keep=rows_type(),
            _send=rows_type(),
        ),
        [
            rows_scratch(),
            rows_scratch(),
            rows_scratch(),
            map_scratch(72),
            map_scratch(72),
            map_scratch(MAP1),
            map_scratch(MAP2),
            map_scratch(FLAT),
            rows_scratch(),
            pltpu.SemaphoreType.DMA((12,)),
        ],
        8,
        f"bwd{moment}",
        4 * ROWS * C * C,
        8 * MIB,
    )


def taps_body(moment, ins, outs, scratch):
    s1, s2, g1, g2, sems = scratch
    out = outs.sums
    pairs = backward_pairs(moment)
    section = lax.axis_index(SECTION)
    active = is_active(section, pairs)

    @pl.when(active)
    def _():
        copies = Copies(sems)
        get = [copies.by_section(section, {s: ins._s2[when] for s, _, when in pairs}, s2)]
        get.append(copies.start(ins._g2, g2))
        later = [copies.by_section(section, {s: ins._s1[when] for s, _, when in pairs}, s1)]
        later.append(copies.start(ins._g1, g1))
        for start, field, grad, dilation, waits in ((9, s2, g2, 2, get), (0, s1, g1, 1, later)):
            for copy in waits:
                copy.wait()
            found = kernel_grad(field, grad, dilation)
            for t in range(9):
                rows = pl.ds(8 * (start + t), 8)
                out[rows, :] = found[t] + (ins.sums[rows, :] if moment > SECTIONS - 1 else 0.0)

    @pl.when(jnp.logical_not(active))
    def _():
        out[...] = ins.sums[...] if moment > SECTIONS - 1 else jnp.zeros_like(out)


def taps(moment, sums, maps1, maps2, g1, g2, after):
    ins = dict(_g1=g1, _g2=g2, _s1={}, _s2={}, _after=after)
    if sums is not None:
        ins.update(sums=sums)
    for s, micro, when in backward_pairs(moment):
        ins["_s1"][when] = maps1[when]
        ins["_s2"][when] = maps2[when]
    return call(
        functools.partial(taps_body, moment),
        ins,
        dict(sums=map_type(18 * GROUPS)),
        [
            map_scratch(MAP1),
            map_scratch(MAP2),
            map_scratch(MAP1),
            map_scratch(MAP2),
            pltpu.SemaphoreType.DMA((4,)),
        ],
        6,
        f"taps{moment}",
        40 * ROWS * C,
        3 * MIB,
    ).sums


QUARTER = C // 4
HALF = QUARTER // 2
SMALL = 16


def places():
    replica = lax.axis_index(REPLICA)
    core = lax.rem(replica, 2)
    x = lax.rem(lax.div(replica, 2), 4)
    y = lax.div(replica, 8)
    return core, jnp.where(core == 0, x, y), jnp.where(core == 0, y, x)


def gather_operands(operands, micros):
    ahead = [m + s for m in micros for s in range(SECTIONS)]
    back = [m + 2 * SECTIONS - 2 - s for m in micros for s in range(SECTIONS)]
    left = [{t: value[t] for t in ahead} for value in operands[:2]]
    right = [{t: value[t] for t in back} for value in operands[2:]]
    return dict(_lefts=left, _rights=right)


def stack_operands(ins, micros, left, right, sems):
    section = lax.axis_index(SECTION)
    for s in range(SECTIONS):

        @pl.when(section == s)
        def _(s=s):
            for n, m in enumerate(micros):
                ahead, back = m + s, m + 2 * SECTIONS - 2 - s
                for h in range(2):
                    k = 2 * n + h
                    rows = pl.ds(k * ROWS, ROWS)
                    a, b = ins._lefts[h][ahead], ins._rights[h][back]
                    pltpu.make_async_copy(a, left.at[rows, :], sems.at[2 * k]).start()
                    pltpu.make_async_copy(b, right.at[rows, :], sems.at[2 * k + 1]).start()

    for k in range(2 * len(micros)):
        rows = pl.ds(k * ROWS, ROWS)
        pltpu.make_async_copy(left.at[rows, :], left.at[rows, :], sems.at[2 * k]).wait()
        pltpu.make_async_copy(right.at[rows, :], right.at[rows, :], sems.at[2 * k + 1]).wait()


def early_body(micros, ins, outs, scratch):
    left, right, sems = scratch
    out = outs.early
    stack_operands(ins, micros, left, right, sems)

    def part(n, carry):
        start = pl.multiple_of(n * QUARTER, QUARTER)
        out[pl.ds(start, QUARTER), :] = dot(left[:, pl.ds(start, QUARTER)], right[...], ((0,), (0,)))
        return carry

    lax.fori_loop(0, 4, part, 0)


def early_weights(operands):
    micros = tuple(range(MICRO - 1))
    size = 2 * len(micros) * ROWS
    return call(
        functools.partial(early_body, micros),
        gather_operands(operands, micros),
        dict(early=jax.ShapeDtypeStruct((C, C), F32)),
        [rows_scratch(size), rows_scratch(size), pltpu.SemaphoreType.DMA((4 * len(micros),))],
        12,
        "early_weights",
        2 * size * C * C,
        8 * MIB,
    ).early


def part_of(early, left, right, number):
    start = pl.multiple_of(lax.rem(number, 4) * QUARTER, QUARTER)
    added = dot(left[:, pl.ds(start, QUARTER)], right[...], ((0,), (0,)))
    return early[pl.ds(start, QUARTER), :] + added


def far_body(ins, outs, scratch):
    (sems,) = scratch
    left, right = outs.left, outs.right
    stack_operands(ins, (MICRO - 1,), left, right, sems)
    _, mine, _ = places()
    whole = part_of(ins.early, left, right, mine + 2).astype(BF)
    outs.up[...] = whole[:HALF]
    outs.low[...] = whole[HALF:]


def far_part(operands, early):
    size = 2 * ROWS
    return call(
        far_body,
        dict(early=early, **gather_operands(operands, (MICRO - 1,))),
        dict(
            up=rows_type(HALF),
            low=rows_type(HALF),
            left=rows_type(size),
            right=rows_type(size),
        ),
        [pltpu.SemaphoreType.DMA((4,))],
        8,
        "far_part",
        2 * size * C * QUARTER,
        3 * MIB,
    )


def tail_body(ins, outs, scratch):
    small, wide = scratch
    both = ins.sums[...] + ins.other[...]
    small[...] = jnp.where(this_core() == 0, both[:72], both[72:])
    wide[...] = jnp.zeros((SMALL, C), F32)
    for g in range(GROUPS):
        wide[pl.ds(0, 9), 128 * g : 128 * (g + 1)] = small[pl.ds(g, 9, stride=GROUPS), :]
    outs.tail[...] = wide[...].astype(BF)


def tail_part(sums, other):
    return call(
        tail_body,
        dict(sums=sums, other=other),
        dict(tail=rows_type(SMALL)),
        [map_scratch(72), pltpu.VMEM((SMALL, C), F32)],
        2,
        "tail",
        0,
        MIB,
    ).tail


def near_body(ins, outs, scratch):
    _, mine, _ = places()
    after = part_of(ins.early, ins.left, ins.right, mine + 1)
    outs.after_up[...] = after[:HALF]
    outs.after_low[...] = after[HALF:].astype(BF)
    before = part_of(ins.early, ins.left, ins.right, mine + 3)
    outs.before_up[...] = before[:HALF].astype(BF)
    outs.before_low[...] = before[HALF:]
    outs.own[...] = part_of(ins.early, ins.left, ins.right, mine)


def wide_type(n):
    return jax.ShapeDtypeStruct((n, C), F32)


def near_parts(early, left, right):
    return call(
        near_body,
        dict(early=early, left=left, right=right),
        dict(
            after_up=wide_type(HALF),
            after_low=rows_type(HALF),
            before_up=rows_type(HALF),
            before_low=wide_type(HALF),
            own=wide_type(QUARTER),
        ),
        [],
        8,
        "near_parts",
        2 * 2 * ROWS * C * QUARTER * 3,
        8 * MIB,
    )


def relay_body(ins, outs, scratch):
    outs.after[...] = (ins.after[...] + ins.up[...].astype(F32)).astype(BF)
    outs.before[...] = (ins.before[...] + ins.low[...].astype(F32)).astype(BF)


def relay(after, before, up, low, waits):
    return call(
        relay_body,
        dict(after=after, before=before, up=up, low=low, _after=waits),
        dict(after=rows_type(HALF), before=rows_type(HALF)),
        [],
        4,
        "relay",
        0,
        4 * MIB,
    )


def mark_body(ins, outs, scratch):
    outs.mark[...] = jnp.zeros_like(outs.mark)


def after_both_cores(values):
    mark = call(mark_body, dict(_after=values), dict(mark=map_type(8)), [], 1, "mark", 0, 4096).mark
    return to_core(mark)


def ring_sum(a, b, c, d):
    a, b, c, d = (value.astype(F32) for value in (a, b, c, d))
    return (a + b) + (c + d)


def first_sum_body(ins, outs, scratch):
    up, low = [a.astype(F32) + b.astype(F32) for a, b in ((ins.ups[0][...], ins.ups[1][...]), (ins.lows[0][...], ins.lows[1][...]))]
    outs.up[pl.ds(0, HALF), :] = (ins.own[:HALF] + up).astype(BF)
    outs.up[pl.ds(HALF, SMALL), :] = ins.tail[...]
    outs.low[...] = (ins.own[HALF:] + low).astype(BF)


def first_sum(own, ups, lows, tail, waits):
    found = call(
        first_sum_body,
        dict(own=own, ups=ups, lows=lows, tail=tail, _after=waits),
        dict(up=rows_type(HALF + SMALL), low=rows_type(HALF)),
        [],
        4,
        "first_sum",
        0,
        4 * MIB,
    )
    return found.up, found.low


def pair_sum_body(ins, outs, scratch):
    outs.up[...] = (ins.up[...].astype(F32) + ins.up_came[...].astype(F32)).astype(BF)
    outs.low[...] = (ins.low[...].astype(F32) + ins.low_came[...].astype(F32)).astype(BF)


def pair_sum(up, low, up_came, low_came, waits):
    found = call(
        pair_sum_body,
        dict(up=up, low=low, up_came=up_came, low_came=low_came, _after=waits),
        dict(up=rows_type(HALF + SMALL), low=rows_type(HALF)),
        [],
        3,
        "pair_sum",
        0,
        2 * MIB,
    )
    return found.up, found.low


def other_a(place):
    return place + 1 - 2 * lax.rem(place, 2)


def other_b(place):
    return 3 - place


def convert(outs, blocks, wide, sems):
    core, mine, its = places()
    waits = []
    for n, (part, low, own, by_a, by_b) in enumerate(blocks):
        place = mine if own else its
        place = other_a(place) if by_a else place
        place = other_b(place) if by_b else place
        slot, sem = wide.at[n], sems.at[n]
        slot[...] = part[pl.ds(0, HALF), :].astype(F32)
        rows = pl.ds(pl.multiple_of(place * QUARTER + low * HALF, HALF), HALF)

        @pl.when(core == (0 if own else 1))
        def _(slot=slot, rows=rows, sem=sem):
            pltpu.make_async_copy(slot, outs._point1.at[0, rows, :], sem).start()

        @pl.when(core == (1 if own else 0))
        def _(slot=slot, rows=rows, sem=sem):
            pltpu.make_async_copy(slot, outs._point2.at[0, rows, :], sem).start()

        waits.append(pltpu.make_async_copy(slot, slot, sem))
    for copy in waits:
        copy.wait()


POINT = jax.ShapeDtypeStruct((1, C, C), F32)


def write_body(kinds, with_tails, ins, outs, scratch):
    if with_tails:
        own, its = [
            ring_sum(*[ins.tails[n][k][pl.ds(HALF, SMALL), :] for k in range(4)])[:9] for n in range(2)
        ]
        core = this_core()
        outs.small1[:, 0, :] = jnp.where(core == 0, own, its)
        outs.small2[:, 0, :] = jnp.where(core == 0, its, own)
    convert(outs, [(ins.parts[n], *kind) for n, kind in enumerate(kinds)], *scratch)


def write(blocks, begun, tails):
    parts = [block[0] for block in blocks]
    ins, outs = dict(parts=parts), dict(_point1=POINT, _point2=POINT)
    aliases = None
    if begun is not None:
        ins.update(_was1=begun._point1, _was2=begun._point2)
        aliases = dict(_was1="_point1", _was2="_point2")
    if tails:
        small = jax.ShapeDtypeStruct((9, 1, C), F32)
        ins.update(tails=tails)
        outs.update(small1=small, small2=small)
    return call(
        functools.partial(write_body, [block[1:] for block in blocks], bool(tails)),
        ins,
        outs,
        [pltpu.VMEM((len(blocks), HALF, C), F32), pltpu.SemaphoreType.DMA((len(blocks),))],
        10,
        "write",
        100 * MIB,
        len(blocks) * HALF * C * 6,
        aliases,
    )


def to_replica(value, target):
    return lax.ppermute(value, REPLICA, [(r, target(r)) for r in range(32)])


def to_core(value):
    return to_replica(value, lambda r: r ^ 1)


def along_x(r, d):
    return (r // 8) * 8 + ((r // 2 + d) % 4) * 2 + r % 2


def along_y(r, d):
    return ((r // 8 + d) % 4) * 8 + r % 8


def along_first(value, d):
    return to_replica(value, lambda r: along_x(r, d) if r % 2 == 0 else along_y(r, d))


def pair_a(value, first):
    return to_pair(value, first, lambda place: place ^ 1)


def pair_b(value, first):
    return to_pair(value, first, lambda place: 3 - place)


def to_pair(value, first, partner):
    def target(r):
        x, y, core = (r // 2) % 4, r // 8, r % 2
        if (core == 0) == first:
            x = partner(x)
        else:
            y = partner(y)
        return y * 8 + x * 2 + core

    return to_replica(value, target)


def to_neighbours(value, pairs, step, swap):
    came = {}
    for source, target in pairs:
        near = min(source, target) % 2 == 0
        if target % 2 not in came and swap:
            places = [(s, s ^ 1 if near else 3 - s) for s in range(SECTIONS)]
            came[target % 2] = lax.ppermute(value, SECTION, places)
    if pairs and not swap:
        places = [(s, s + step) for s in range(SECTIONS) if 0 <= s + step < SECTIONS]
        came[0] = came[1] = lax.ppermute(value, SECTION, places)
    return came


def per_device(images, cotangent, depth_first, point_first, depth_second, point_second):
    images = images.reshape(MICRO, ROWS, C)
    cotangent = cotangent.reshape(MICRO, ROWS, C)
    weights = (depth_first[0], depth_second[0], point_first[0], point_second[0])
    xs, projs, maps1, maps2 = {}, {}, {}, {}
    operands = ({}, {}, {}, {})
    grads1, grads2 = {}, {}
    came, returned = {}, {}
    sums = early = None
    last = 3 * SECTIONS - 3
    full = MICRO + SECTIONS - 2
    for moment in range(last + 1):
        if moment <= full:
            after = [operands[1][moment - 2]] if 1 < moment < MICRO else []
            if moment == 2:
                after += back_weights[2:]
            found = forward(moment, images, came, *weights, after)
            maps1[moment], maps2[moment] = found._map1, found._map2
            projs[moment] = found._proj
            if moment > 0:
                xs[moment] = found._x
            operands[0][moment] = found._keep
            if moment == 0:
                back_weights = [*weights[:2], *turned(*weights[2:], [found._keep])]
            operands[1][moment] = to_core(found._send)
            going = [(s, s + 1) for s in forward_sections(moment) if s < SECTIONS - 1]
            came = to_neighbours(found.x, sorted(going, reverse=True), 1, moment < SECTIONS - 1)
        if moment >= SECTIONS - 1:
            after = [] if sums is None else [sums]
            after += [] if early is None else [early]
            if moment == full + 1:
                after += [operands[1][past] for past in range(MICRO - 2, full + 1)]
            if moment == full + 2:
                after += [operands[3][past] for past in range(SECTIONS - 1, full + 1)]
            found = backward(moment, cotangent, returned, xs, projs, *back_weights, after)
            grads2[moment], grads1[moment] = found._map2, found._map1
            operands[2][moment] = found._keep
            operands[3][moment] = to_core(found._send)
            going = [(s, s - 1) for s, _, _ in backward_pairs(moment) if s > 0]
            returned = to_neighbours(found.g, sorted(going, reverse=True), -1, moment >= full)
        if full <= moment < last:
            for past in range(SECTIONS - 1, moment + 1) if moment == full else [moment]:
                sums = taps(past, sums, maps1, maps2, grads1[past], grads2[past], [grads1[moment]])
        if moment == last - 1:
            early = early_weights(operands)
    far = far_part(operands, early)
    sums = taps(last, sums, maps1, maps2, grads1[last], grads2[last], [far.left])
    up, low = along_first(far.up, 1), along_first(far.low, -1)
    near = near_parts(early, far.left, far.right)
    near_low, near_up = along_first(near.after_low, 1), along_first(near.before_up, -1)
    sent = relay(near.after_up, near.before_low, up, low, [sums])
    tail = tail_part(sums, to_core(sums))
    up, low = along_first(sent.after, 1), along_first(sent.before, -1)
    both = after_both_cores([up, low])
    up, low = first_sum(near.own, [up, near_up], [near_low, low], tail, [both])
    up, low = pair_sum(up, low, pair_a(up, False), pair_b(low, False), [])
    up_came, low_came = pair_b(up, False), pair_a(low, False)
    both = after_both_cores([up_came, low_came])
    up, low = pair_sum(up, low, up_came, low_came, [both])
    up_a, low_b = pair_a(up, True), pair_b(low, True)
    up_b, low_a = pair_b(up, True), pair_a(low, True)
    up_ab, low_ab = pair_b(up_a, True), pair_a(low_b, True)
    own = [[up, up_a, up_ab, up_b], [low, low_a, low_ab, low_b]]
    its = [[to_core(value) for value in values] for values in own]
    came = ((0, 0), (1, 0), (1, 1), (0, 1))
    blocks = [
        (values[low][n], low, values is own, *came[n])
        for values in (own, its)
        for n in (0, 1, 3, 2)
        for low in (0, 1)
    ]
    late = [block for block in blocks if block[3:] == (1, 1)]
    begun = write([block for block in blocks if block[3:] != (1, 1)], None, None)
    done = write(late, begun, [own[0], its[0]])
    small1, small2 = jnp.swapaxes(done.small1, 0, 1), jnp.swapaxes(done.small2, 0, 1)
    return small1, done._point1, small2, done._point2


def solution(mesh):
    sharded = P(None, REPLICA, None, None, None)
    by_section = P(SECTION, None, None)
    return jax.shard_map(
        per_device,
        mesh=mesh,
        in_specs=(sharded, sharded) + (by_section,) * 4,
        out_specs=(by_section,) * 4,
        check_vma=False,
    )
```

```python
import functools
from types import SimpleNamespace

import jax
import jax.numpy as jnp
from jax import lax
from jax.experimental import pallas as pl
from jax.experimental.pallas import tpu as pltpu
from jax.sharding import PartitionSpec as P

BF = jnp.bfloat16
F32 = jnp.float32
SIDE = 12
ROWS = SIDE * SIDE
C = 1024
GROUPS = C // 128
LINE = SIDE * GROUPS
MICRO = 4
SECTIONS = 4
MAP1 = (SIDE + 2) * LINE
MAP2 = (SIDE + 4) * LINE
FLAT = SIDE * LINE
MIB = 1024 * 1024
SECTION = "section"
REPLICA = "replica"

ANY = pl.BlockSpec(memory_space=pl.ANY)
VM = pl.BlockSpec(memory_space=pltpu.VMEM)


def sigmoid(v):
    return 0.5 * jnp.tanh(0.5 * v) + 0.5


def slope(v):
    s = sigmoid(v)
    return s * (1.0 + v * (1.0 - s))


def widen_kernel(k_ref, wide):
    for g in range(GROUPS):
        wide[pl.ds(g, 9, stride=GROUPS), :] = k_ref[:, 128 * g : 128 * (g + 1)].astype(F32)


def clear_edges(field, dilation):
    size = dilation * LINE
    zero = jnp.zeros((size, 128), F32)
    field[pl.ds(0, size), :] = zero
    field[pl.ds(FLAT + size, size), :] = zero


def depthwise(field, wide, out, dilation, flip):
    taps = [wide[pl.ds(8 * (8 - t if flip else t), 8), :] for t in range(9)]

    def line(i, carry):
        seen = {}

        def at(p, j):
            if (p, j) not in seen:
                start = pl.multiple_of((i + p * dilation) * LINE + j * GROUPS, 8)
                seen[p, j] = field[pl.ds(start, 8), :]
            return seen[p, j]

        for j in range(SIDE):
            total = None
            for t in range(9):
                p, q = divmod(t, 3)
                col = j + (q - 1) * dilation
                if 0 <= col < SIDE:
                    term = taps[t] * at(p, col)
                    total = term if total is None else total + term
            out[pl.ds(pl.multiple_of(i * LINE + j * GROUPS, 8), 8), :] = total
        return carry

    lax.fori_loop(0, SIDE, line, 0)


def kernel_grad(field, grad, dilation):
    def line(i, sums):
        sums = list(sums)
        seen = {}

        def at(p, j):
            if (p, j) not in seen:
                start = pl.multiple_of((i + p * dilation) * LINE + j * GROUPS, 8)
                seen[p, j] = field[pl.ds(start, 8), :]
            return seen[p, j]

        for j in range(SIDE):
            here = grad[pl.ds(pl.multiple_of((i + dilation) * LINE + j * GROUPS, 8), 8), :]
            for t in range(9):
                p, q = divmod(t, 3)
                col = j + (q - 1) * dilation
                if 0 <= col < SIDE:
                    sums[t] = sums[t] + here * at(p, col)
        return tuple(sums)

    return lax.fori_loop(0, SIDE, line, tuple(jnp.zeros((8, 128), F32) for _ in range(9)))


def rows_to_map(field, base, p, g, value):
    field[pl.ds(base + 16 * p * GROUPS + g, 16, stride=GROUPS), :] = value


def map_to_rows(field, p, g):
    return field[pl.ds(16 * p * GROUPS + g, 16, stride=GROUPS), :]


def tiles(body):
    def step(p, carry):
        for g in range(GROUPS):
            body(p, g, pl.ds(pl.multiple_of(16 * p, 16), 16), pl.ds(128 * g, 128))
        return carry

    lax.fori_loop(0, ROWS // 16, step, 0)


def dot(a, b, dims):
    return lax.dot_general(a, b, (dims, ((), ())), preferred_element_type=F32)


def rows_type(n=ROWS):
    return jax.ShapeDtypeStruct((n, C), BF)


def map_type(n):
    return jax.ShapeDtypeStruct((n, 128), F32)


def call(body, ins, outs, scratch, limit, name, flops, size, aliases=None):
    flat, tree = jax.tree.flatten(ins)
    out_flat, out_tree = jax.tree.flatten(outs)

    def kernel(*refs):
        first, last = len(flat), len(flat) + len(out_flat)
        given = SimpleNamespace(**jax.tree.unflatten(tree, refs[:first]))
        made = SimpleNamespace(**jax.tree.unflatten(out_tree, refs[first:last]))
        body(given, made, refs[last:])

    def names(arrays):
        return jax.tree.leaves({n: jax.tree.map(lambda _: n, value) for n, value in arrays.items()})

    def specs(arrays):
        return [ANY if n.startswith("_") else VM for n in names(arrays)]

    found = pl.pallas_call(
        kernel,
        out_shape=out_flat,
        in_specs=specs(ins),
        out_specs=specs(outs),
        scratch_shapes=scratch,
        input_output_aliases={
            names(ins).index(a): names(outs).index(b) for a, b in (aliases or {}).items()
        },
        compiler_params=pltpu.CompilerParams(vmem_limit_bytes=limit * MIB),
        cost_estimate=pl.CostEstimate(flops=flops, bytes_accessed=size, transcendentals=0),
        name=name,
    )(*flat)
    return SimpleNamespace(**jax.tree.unflatten(out_tree, found))


class Copies:
    def __init__(self, sems):
        self.sems = sems
        self.count = 0

    def next(self):
        self.count += 1
        return self.sems.at[self.count - 1]

    def start(self, source, target):
        copy = pltpu.make_async_copy(source, target, self.next())
        copy.start()
        return copy

    def by_section(self, section, choices, target):
        sem = self.next()
        for s, source in choices.items():

            @pl.when(section == s)
            def _(source=source):
                pltpu.make_async_copy(source, target, sem).start()

        return pltpu.make_async_copy(target, target, sem)

    def by_core(self, core, value, on_zero, on_one):
        sem = self.next()

        @pl.when(core == 0)
        def _():
            pltpu.make_async_copy(value, on_zero, sem).start()

        @pl.when(core == 1)
        def _():
            pltpu.make_async_copy(value, on_one, sem).start()

        return pltpu.make_async_copy(value, value, sem)


def this_core():
    return lax.rem(lax.axis_index(REPLICA), 2)


def rows_scratch(n=ROWS):
    return pltpu.VMEM((n, C), BF)


def map_scratch(n):
    return pltpu.VMEM((n, 128), F32)


def pick(section, target, choices):
    if len(choices) == 1:
        return next(iter(choices.values()))
    for s, ref in choices.items():

        @pl.when(section == s)
        def _(ref=ref):
            target[...] = ref[...]

    return target


def forward_sections(moment):
    return [s for s in range(SECTIONS) if 0 <= moment - s < MICRO]


def forward_body(moment, ins, outs, scratch):
    xs, wide1, wide2, map1, map2, work, fv, sv, pv, sems, *own = scratch
    section = lax.axis_index(SECTION)
    core = this_core()
    slot = moment - section

    @pl.when((slot >= 0) & (slot < MICRO))
    def _():
        copies = Copies(sems)
        x_out = outs.x
        if moment < MICRO:
            get_x = pltpu.make_async_copy(ins._images.at[moment], xs, copies.next())
            pl.when(section == 0)(get_x.start)
        puts = []
        if own:
            w1, w2 = own
            gets = [copies.start(ins._p1, w1), copies.start(ins._p2, w2)]
        else:
            w1, w2 = ins.p1, ins.p2
        widen_kernel(ins.k1, wide1)
        widen_kernel(ins.k2, wide2)
        clear_edges(map1, 1)
        clear_edges(map2, 2)
        if moment < MICRO:
            pl.when(section == 0)(get_x.wait)
        came = {s: ins.came[s % 2] for s in forward_sections(moment) if s > 0}
        if moment < MICRO and moment > 0:
            came[0] = xs
            for s, ref in came.items():
                if s > 0:

                    @pl.when(section == s)
                    def _(ref=ref):
                        xs[...] = ref[...]

        xv = xs if moment < MICRO else pick(section, xs, came)
        if moment > 0:
            puts.append(copies.start(xv, outs._x))

        def enter(p, g, rows, cols):
            v = xv[rows, cols].astype(F32)
            rows_to_map(map1, LINE, p, g, v * sigmoid(v))

        tiles(enter)
        depthwise(map1, wide1, work, 1, False)

        def collect_first(p, g, rows, cols):
            fv[rows, cols] = map_to_rows(work, p, g).astype(BF)

        tiles(collect_first)
        if own:
            for get in gets:
                get.wait()
        puts.append(copies.start(map1, outs._map1))
        puts.append(copies.by_core(core, fv, outs._keep, outs._send))
        for n in range(4):
            cols = pl.ds(256 * n, 256)
            pre = dot(fv[...], w1[:, cols], ((1,), (0,)))
            pv[:, cols] = pre.astype(BF)
            hidden = (pre * sigmoid(pre)).astype(BF).astype(F32)
            for g in range(2):
                map2[pl.ds(2 * LINE + 2 * n + g, ROWS, stride=GROUPS), :] = hidden[
                    :, 128 * g : 128 * (g + 1)
                ]
        puts.append(copies.start(pv, outs._proj))
        puts.append(copies.start(map2, outs._map2))
        depthwise(map2, wide2, work, 2, False)

        def collect_second(p, g, rows, cols):
            sv[rows, cols] = map_to_rows(work, p, g).astype(BF)

        tiles(collect_second)
        puts.append(copies.by_core(core, sv, outs._send, outs._keep))

        @pl.when(section != SECTIONS - 1)
        def _():
            for n in range(4):
                cols = pl.ds(256 * n, 256)
                branch = dot(sv[...], w2[:, cols], ((1,), (0,)))
                x_out[:, cols] = (xv[:, cols].astype(F32) + branch).astype(BF)

        for put in puts:
            put.wait()


def forward(moment, images, came, k1, k2, p1, p2, after):
    ins = dict(k1=k1, k2=k2, came=came, _after=after)
    ins.update(dict(p1=p1, p2=p2) if moment > 0 else dict(_p1=p1, _p2=p2))
    outs = dict(
        x=rows_type(),
        _map1=map_type(MAP1),
        _map2=map_type(MAP2),
        _proj=rows_type(),
        _keep=rows_type(),
        _send=rows_type(),
    )
    if moment < MICRO:
        ins.update(_images=images)
    if moment > 0:
        outs.update(_x=rows_type())
    return call(
        functools.partial(forward_body, moment),
        ins,
        outs,
        [
            rows_scratch(),
            map_scratch(72),
            map_scratch(72),
            map_scratch(MAP1),
            map_scratch(MAP2),
            map_scratch(FLAT),
            rows_scratch(),
            rows_scratch(),
            rows_scratch(),
            pltpu.SemaphoreType.DMA((10,)),
            *([rows_scratch(C), rows_scratch(C)] if moment == 0 else []),
        ],
        8 if moment > 0 else 14,
        f"fwd{moment}",
        4 * ROWS * C * C,
        8 * MIB,
    )


def turn_body(ins, outs, scratch):
    for out, value in ((outs.p1, ins.p1), (outs.p2, ins.p2)):
        for n in range(4):
            for m in range(4):
                rows, cols = pl.ds(256 * n, 256), pl.ds(256 * m, 256)
                out[cols, rows] = value[rows, cols].T


def turned(p1, p2, after):
    square = rows_type(C)
    found = call(
        turn_body,
        dict(p1=p1, p2=p2, _after=after),
        dict(p1=square, p2=square),
        [],
        8,
        "turn",
        100 * MIB,
        8 * MIB,
    )
    return found.p1, found.p2


def backward_pairs(moment):
    found = []
    for section in range(SECTIONS):
        micro = moment - (2 * SECTIONS - 2) + section
        if 0 <= micro < MICRO:
            found.append((section, micro, micro + section))
    return found


def is_active(section, pairs):
    return functools.reduce(lambda a, b: a | b, [section == s for s, _, _ in pairs])


def backward_body(moment, ins, outs, scratch):
    gs, xs, ps, wide1, wide2, map1, map2, work, hv, sems = scratch
    pairs = backward_pairs(moment)
    section = lax.axis_index(SECTION)
    core = this_core()

    @pl.when(is_active(section, pairs))
    def _():
        copies = Copies(sems)
        g_out = outs.g
        top = [micro for s, micro, _ in pairs if s == SECTIONS - 1]
        if top:
            get_g = pltpu.make_async_copy(ins._cotangent.at[top[0]], gs, copies.next())
            pl.when(section == SECTIONS - 1)(get_g.start)
        parts = [pl.ds(QUARTER * n, QUARTER) for n in range(4)]
        get_p = copies.by_section(section, {s: ins._proj[when] for s, _, when in pairs}, ps)
        get_x = copies.by_section(section, {s: ins._x[when] for s, _, when in pairs if s > 0}, xs)
        widen_kernel(ins.k1, wide1)
        widen_kernel(ins.k2, wide2)
        clear_edges(map1, 1)
        clear_edges(map2, 2)
        came = {s: ins.came[s % 2] for s, _, _ in pairs if s < SECTIONS - 1}
        if top:
            pl.when(section == SECTIONS - 1)(get_g.wait)
            for s, ref in came.items():

                @pl.when(section == s)
                def _(ref=ref):
                    gs[...] = ref[...]

        gv = gs if top else pick(section, gs, came)
        for n in range(4):
            part = dot(gv[...], ins.p2[:, parts[n]], ((1,), (0,)))
            part = part.astype(BF).astype(F32)
            for g in range(2):
                map2[pl.ds(2 * LINE + 2 * n + g, ROWS, stride=GROUPS), :] = part[
                    :, 128 * g : 128 * (g + 1)
                ]
        puts = [copies.by_core(core, gv, outs._send, outs._keep)]
        puts.append(copies.start(map2, outs._map2))
        depthwise(map2, wide2, work, 2, True)
        get_p.wait()

        def collect_hidden(p, g, rows, cols):
            hv[rows, cols] = (map_to_rows(work, p, g) * slope(ps[rows, cols].astype(F32))).astype(BF)

        tiles(collect_hidden)
        puts.append(copies.by_core(core, hv, outs._keep, outs._send))
        for n in range(4):
            part = dot(hv[...], ins.p1[:, parts[n]], ((1,), (0,)))
            part = part.astype(BF).astype(F32)
            for g in range(2):
                map1[pl.ds(LINE + 2 * n + g, ROWS, stride=GROUPS), :] = part[
                    :, 128 * g : 128 * (g + 1)
                ]
        puts.append(copies.start(map1, outs._map1))

        @pl.when(section != 0)
        def _():
            get_x.wait()
            depthwise(map1, wide1, work, 1, True)

            def collect(p, g, rows, cols):
                back = map_to_rows(work, p, g) * slope(xs[rows, cols].astype(F32))
                g_out[rows, cols] = (gv[rows, cols].astype(F32) + back).astype(BF)

            tiles(collect)

        for put in puts:
            put.wait()


def backward(moment, cotangent, came, xs, projs, k1, k2, p1, p2, after):
    ins = dict(k1=k1, k2=k2, p1=p1, p2=p2, _x={}, _proj={}, _after=after, came=came)
    for s, micro, when in backward_pairs(moment):
        if s == SECTIONS - 1:
            ins.update(_cotangent=cotangent)
        if s > 0:
            ins["_x"][when] = xs[when]
        ins["_proj"][when] = projs[when]
    return call(
        functools.partial(backward_body, moment),
        ins,
        dict(
            g=rows_type(),
            _map2=map_type(MAP2),
            _map1=map_type(MAP1),
            _keep=rows_type(),
            _send=rows_type(),
        ),
        [
            rows_scratch(),
            rows_scratch(),
            rows_scratch(),
            map_scratch(72),
            map_scratch(72),
            map_scratch(MAP1),
            map_scratch(MAP2),
            map_scratch(FLAT),
            rows_scratch(),
            pltpu.SemaphoreType.DMA((12,)),
        ],
        8,
        f"bwd{moment}",
        4 * ROWS * C * C,
        8 * MIB,
    )


def taps_body(moment, ins, outs, scratch):
    s1, s2, g1, g2, sems = scratch
    out = outs.sums
    pairs = backward_pairs(moment)
    section = lax.axis_index(SECTION)
    active = is_active(section, pairs)

    @pl.when(active)
    def _():
        copies = Copies(sems)
        get = [copies.by_section(section, {s: ins._s2[when] for s, _, when in pairs}, s2)]
        get.append(copies.start(ins._g2, g2))
        later = [copies.by_section(section, {s: ins._s1[when] for s, _, when in pairs}, s1)]
        later.append(copies.start(ins._g1, g1))
        for start, field, grad, dilation, waits in ((9, s2, g2, 2, get), (0, s1, g1, 1, later)):
            for copy in waits:
                copy.wait()
            found = kernel_grad(field, grad, dilation)
            for t in range(9):
                rows = pl.ds(8 * (start + t), 8)
                out[rows, :] = found[t] + (ins.sums[rows, :] if moment > SECTIONS - 1 else 0.0)

    @pl.when(jnp.logical_not(active))
    def _():
        out[...] = ins.sums[...] if moment > SECTIONS - 1 else jnp.zeros_like(out)


def taps(moment, sums, maps1, maps2, g1, g2, after):
    ins = dict(_g1=g1, _g2=g2, _s1={}, _s2={}, _after=after)
    if sums is not None:
        ins.update(sums=sums)
    for s, micro, when in backward_pairs(moment):
        ins["_s1"][when] = maps1[when]
        ins["_s2"][when] = maps2[when]
    return call(
        functools.partial(taps_body, moment),
        ins,
        dict(sums=map_type(18 * GROUPS)),
        [
            map_scratch(MAP1),
            map_scratch(MAP2),
            map_scratch(MAP1),
            map_scratch(MAP2),
            pltpu.SemaphoreType.DMA((4,)),
        ],
        6,
        f"taps{moment}",
        40 * ROWS * C,
        3 * MIB,
    ).sums


QUARTER = C // 4
HALF = QUARTER // 2
SMALL = 16


def places():
    replica = lax.axis_index(REPLICA)
    core = lax.rem(replica, 2)
    x = lax.rem(lax.div(replica, 2), 4)
    y = lax.div(replica, 8)
    return core, jnp.where(core == 0, x, y), jnp.where(core == 0, y, x)


def gather_operands(operands, micros):
    ahead = [m + s for m in micros for s in range(SECTIONS)]
    back = [m + 2 * SECTIONS - 2 - s for m in micros for s in range(SECTIONS)]
    left = [{t: value[t] for t in ahead} for value in operands[:2]]
    right = [{t: value[t] for t in back} for value in operands[2:]]
    return dict(_lefts=left, _rights=right)


def stack_operands(ins, micros, left, right, sems):
    section = lax.axis_index(SECTION)
    for s in range(SECTIONS):

        @pl.when(section == s)
        def _(s=s):
            for n, m in enumerate(micros):
                ahead, back = m + s, m + 2 * SECTIONS - 2 - s
                for h in range(2):
                    k = 2 * n + h
                    rows = pl.ds(k * ROWS, ROWS)
                    a, b = ins._lefts[h][ahead], ins._rights[h][back]
                    pltpu.make_async_copy(a, left.at[rows, :], sems.at[2 * k]).start()
                    pltpu.make_async_copy(b, right.at[rows, :], sems.at[2 * k + 1]).start()

    for k in range(2 * len(micros)):
        rows = pl.ds(k * ROWS, ROWS)
        pltpu.make_async_copy(left.at[rows, :], left.at[rows, :], sems.at[2 * k]).wait()
        pltpu.make_async_copy(right.at[rows, :], right.at[rows, :], sems.at[2 * k + 1]).wait()


def early_body(micros, ins, outs, scratch):
    left, right, sems = scratch
    out = outs.early
    stack_operands(ins, micros, left, right, sems)

    def part(n, carry):
        start = pl.multiple_of(n * QUARTER, QUARTER)
        out[pl.ds(start, QUARTER), :] = dot(left[:, pl.ds(start, QUARTER)], right[...], ((0,), (0,)))
        return carry

    lax.fori_loop(0, 4, part, 0)


def early_weights(operands):
    micros = tuple(range(MICRO - 1))
    size = 2 * len(micros) * ROWS
    return call(
        functools.partial(early_body, micros),
        gather_operands(operands, micros),
        dict(early=jax.ShapeDtypeStruct((C, C), F32)),
        [rows_scratch(size), rows_scratch(size), pltpu.SemaphoreType.DMA((4 * len(micros),))],
        12,
        "early_weights",
        2 * size * C * C,
        8 * MIB,
    ).early


def part_of(early, left, right, number):
    start = pl.multiple_of(lax.rem(number, 4) * QUARTER, QUARTER)
    added = dot(left[:, pl.ds(start, QUARTER)], right[...], ((0,), (0,)))
    return early[pl.ds(start, QUARTER), :] + added


def far_body(ins, outs, scratch):
    (sems,) = scratch
    left, right = outs.left, outs.right
    stack_operands(ins, (MICRO - 1,), left, right, sems)
    _, mine, _ = places()
    whole = part_of(ins.early, left, right, mine + 2).astype(BF)
    outs.up[...] = whole[:HALF]
    outs.low[...] = whole[HALF:]


def far_part(operands, early):
    size = 2 * ROWS
    return call(
        far_body,
        dict(early=early, **gather_operands(operands, (MICRO - 1,))),
        dict(
            up=rows_type(HALF),
            low=rows_type(HALF),
            left=rows_type(size),
            right=rows_type(size),
        ),
        [pltpu.SemaphoreType.DMA((4,))],
        8,
        "far_part",
        2 * size * C * QUARTER,
        3 * MIB,
    )


def tail_body(ins, outs, scratch):
    small, wide = scratch
    both = ins.sums[...] + ins.other[...]
    small[...] = jnp.where(this_core() == 0, both[:72], both[72:])
    wide[...] = jnp.zeros((SMALL, C), F32)
    for g in range(GROUPS):
        wide[pl.ds(0, 9), 128 * g : 128 * (g + 1)] = small[pl.ds(g, 9, stride=GROUPS), :]
    outs.tail[...] = wide[...].astype(BF)


def tail_part(sums, other):
    return call(
        tail_body,
        dict(sums=sums, other=other),
        dict(tail=rows_type(SMALL)),
        [map_scratch(72), pltpu.VMEM((SMALL, C), F32)],
        2,
        "tail",
        0,
        MIB,
    ).tail


def near_body(ins, outs, scratch):
    _, mine, _ = places()
    after = part_of(ins.early, ins.left, ins.right, mine + 1)
    outs.after_up[...] = after[:HALF]
    outs.after_low[...] = after[HALF:].astype(BF)
    before = part_of(ins.early, ins.left, ins.right, mine + 3)
    outs.before_up[...] = before[:HALF].astype(BF)
    outs.before_low[...] = before[HALF:]
    outs.own[...] = part_of(ins.early, ins.left, ins.right, mine)


def wide_type(n):
    return jax.ShapeDtypeStruct((n, C), F32)


def near_parts(early, left, right):
    return call(
        near_body,
        dict(early=early, left=left, right=right),
        dict(
            after_up=wide_type(HALF),
            after_low=rows_type(HALF),
            before_up=rows_type(HALF),
            before_low=wide_type(HALF),
            own=wide_type(QUARTER),
        ),
        [],
        8,
        "near_parts",
        2 * 2 * ROWS * C * QUARTER * 3,
        8 * MIB,
    )


def relay_body(ins, outs, scratch):
    outs.after[...] = (ins.after[...] + ins.up[...].astype(F32)).astype(BF)
    outs.before[...] = (ins.before[...] + ins.low[...].astype(F32)).astype(BF)


def relay(after, before, up, low, waits):
    return call(
        relay_body,
        dict(after=after, before=before, up=up, low=low, _after=waits),
        dict(after=rows_type(HALF), before=rows_type(HALF)),
        [],
        4,
        "relay",
        0,
        4 * MIB,
    )


def mark_body(ins, outs, scratch):
    outs.mark[...] = jnp.zeros_like(outs.mark)


def after_both_cores(values):
    mark = call(mark_body, dict(_after=values), dict(mark=map_type(8)), [], 1, "mark", 0, 4096).mark
    return to_core(mark)


def ring_sum(a, b, c, d):
    a, b, c, d = (value.astype(F32) for value in (a, b, c, d))
    return (a + b) + (c + d)


def first_sum_body(ins, outs, scratch):
    up, low = [a.astype(F32) + b.astype(F32) for a, b in ((ins.ups[0][...], ins.ups[1][...]), (ins.lows[0][...], ins.lows[1][...]))]
    outs.up[pl.ds(0, HALF), :] = (ins.own[:HALF] + up).astype(BF)
    outs.up[pl.ds(HALF, SMALL), :] = ins.tail[...]
    outs.low[...] = (ins.own[HALF:] + low).astype(BF)


def first_sum(own, ups, lows, tail, waits):
    found = call(
        first_sum_body,
        dict(own=own, ups=ups, lows=lows, tail=tail, _after=waits),
        dict(up=rows_type(HALF + SMALL), low=rows_type(HALF)),
        [],
        4,
        "first_sum",
        0,
        4 * MIB,
    )
    return found.up, found.low


def pair_sum_body(ins, outs, scratch):
    outs.up[...] = (ins.up[...].astype(F32) + ins.up_came[...].astype(F32)).astype(BF)
    outs.low[...] = (ins.low[...].astype(F32) + ins.low_came[...].astype(F32)).astype(BF)


def pair_sum(up, low, up_came, low_came, waits):
    found = call(
        pair_sum_body,
        dict(up=up, low=low, up_came=up_came, low_came=low_came, _after=waits),
        dict(up=rows_type(HALF + SMALL), low=rows_type(HALF)),
        [],
        3,
        "pair_sum",
        0,
        2 * MIB,
    )
    return found.up, found.low


def other_a(place):
    return place + 1 - 2 * lax.rem(place, 2)


def other_b(place):
    return 3 - place


def convert(outs, blocks, wide, sems):
    core, mine, its = places()
    waits = []
    for n, (part, low, own, by_a, by_b) in enumerate(blocks):
        place = mine if own else its
        place = other_a(place) if by_a else place
        place = other_b(place) if by_b else place
        slot, sem = wide.at[n], sems.at[n]
        slot[...] = part[pl.ds(0, HALF), :].astype(F32)
        rows = pl.ds(pl.multiple_of(place * QUARTER + low * HALF, HALF), HALF)

        @pl.when(core == (0 if own else 1))
        def _(slot=slot, rows=rows, sem=sem):
            pltpu.make_async_copy(slot, outs._point1.at[0, rows, :], sem).start()

        @pl.when(core == (1 if own else 0))
        def _(slot=slot, rows=rows, sem=sem):
            pltpu.make_async_copy(slot, outs._point2.at[0, rows, :], sem).start()

        waits.append(pltpu.make_async_copy(slot, slot, sem))
    for copy in waits:
        copy.wait()


POINT = jax.ShapeDtypeStruct((1, C, C), F32)


def write_body(kinds, with_tails, ins, outs, scratch):
    if with_tails:
        own, its = [
            ring_sum(*[ins.tails[n][k][pl.ds(HALF, SMALL), :] for k in range(4)])[:9] for n in range(2)
        ]
        core = this_core()
        outs.small1[:, 0, :] = jnp.where(core == 0, own, its)
        outs.small2[:, 0, :] = jnp.where(core == 0, its, own)
    convert(outs, [(ins.parts[n], *kind) for n, kind in enumerate(kinds)], *scratch)


def write(blocks, begun, tails):
    parts = [block[0] for block in blocks]
    ins, outs = dict(parts=parts), dict(_point1=POINT, _point2=POINT)
    aliases = None
    if begun is not None:
        ins.update(_was1=begun._point1, _was2=begun._point2)
        aliases = dict(_was1="_point1", _was2="_point2")
    if tails:
        small = jax.ShapeDtypeStruct((9, 1, C), F32)
        ins.update(tails=tails)
        outs.update(small1=small, small2=small)
    return call(
        functools.partial(write_body, [block[1:] for block in blocks], bool(tails)),
        ins,
        outs,
        [pltpu.VMEM((len(blocks), HALF, C), F32), pltpu.SemaphoreType.DMA((len(blocks),))],
        10,
        "write",
        100 * MIB,
        len(blocks) * HALF * C * 6,
        aliases,
    )


def to_replica(value, target):
    return lax.ppermute(value, REPLICA, [(r, target(r)) for r in range(32)])


def to_core(value):
    return to_replica(value, lambda r: r ^ 1)


def along_x(r, d):
    return (r // 8) * 8 + ((r // 2 + d) % 4) * 2 + r % 2


def along_y(r, d):
    return ((r // 8 + d) % 4) * 8 + r % 8


def along_first(value, d):
    return to_replica(value, lambda r: along_x(r, d) if r % 2 == 0 else along_y(r, d))


def pair_a(value, first):
    return to_pair(value, first, lambda place: place ^ 1)


def pair_b(value, first):
    return to_pair(value, first, lambda place: 3 - place)


def to_pair(value, first, partner):
    def target(r):
        x, y, core = (r // 2) % 4, r // 8, r % 2
        if (core == 0) == first:
            x = partner(x)
        else:
            y = partner(y)
        return y * 8 + x * 2 + core

    return to_replica(value, target)


def to_neighbours(value, pairs, step, swap):
    came = {}
    for source, target in pairs:
        near = min(source, target) % 2 == 0
        if target % 2 not in came and swap:
            places = [(s, s ^ 1 if near else 3 - s) for s in range(SECTIONS)]
            came[target % 2] = lax.ppermute(value, SECTION, places)
    if pairs and not swap:
        places = [(s, s + step) for s in range(SECTIONS) if 0 <= s + step < SECTIONS]
        came[0] = came[1] = lax.ppermute(value, SECTION, places)
    return came


def per_device(images, cotangent, depth_first, point_first, depth_second, point_second):
    images = images.reshape(MICRO, ROWS, C)
    cotangent = cotangent.reshape(MICRO, ROWS, C)
    weights = (depth_first[0], depth_second[0], point_first[0], point_second[0])
    xs, projs, maps1, maps2 = {}, {}, {}, {}
    operands = ({}, {}, {}, {})
    grads1, grads2 = {}, {}
    came, returned = {}, {}
    sums = early = None
    last = 3 * SECTIONS - 3
    full = MICRO + SECTIONS - 2
    for moment in range(last + 1):
        if moment <= full:
            after = [operands[1][moment - 2]] if 1 < moment < MICRO else []
            if moment == 2:
                after += back_weights[2:]
            found = forward(moment, images, came, *weights, after)
            maps1[moment], maps2[moment] = found._map1, found._map2
            projs[moment] = found._proj
            if moment > 0:
                xs[moment] = found._x
            operands[0][moment] = found._keep
            if moment == 0:
                back_weights = [*weights[:2], *turned(*weights[2:], [found._keep])]
            operands[1][moment] = to_core(found._send)
            going = [(s, s + 1) for s in forward_sections(moment) if s < SECTIONS - 1]
            came = to_neighbours(found.x, sorted(going, reverse=True), 1, moment < SECTIONS - 1)
        if moment >= SECTIONS - 1:
            after = [] if sums is None else [sums]
            after += [] if early is None else [early]
            if moment == full + 1:
                after += [operands[1][past] for past in range(MICRO - 2, full + 1)]
            if moment == full + 2:
                after += [operands[3][past] for past in range(SECTIONS - 1, full + 1)]
            found = backward(moment, cotangent, returned, xs, projs, *back_weights, after)
            grads2[moment], grads1[moment] = found._map2, found._map1
            operands[2][moment] = found._keep
            operands[3][moment] = to_core(found._send)
            going = [(s, s - 1) for s, _, _ in backward_pairs(moment) if s > 0]
            returned = to_neighbours(found.g, sorted(going, reverse=True), -1, moment >= full)
        if full <= moment < last:
            for past in range(SECTIONS - 1, moment + 1) if moment == full else [moment]:
                sums = taps(past, sums, maps1, maps2, grads1[past], grads2[past], [grads1[moment]])
        if moment == last - 1:
            early = early_weights(operands)
    far = far_part(operands, early)
    sums = taps(last, sums, maps1, maps2, grads1[last], grads2[last], [far.left])
    up, low = along_first(far.up, 1), along_first(far.low, -1)
    near = near_parts(early, far.left, far.right)
    near_low, near_up = along_first(near.after_low, 1), along_first(near.before_up, -1)
    sent = relay(near.after_up, near.before_low, up, low, [sums])
    tail = tail_part(sums, to_core(sums))
    up, low = along_first(sent.after, 1), along_first(sent.before, -1)
    up, low = first_sum(near.own, [up, near_up], [near_low, low], tail, [])
    up, low = pair_sum(up, low, pair_a(up, False), pair_b(low, False), [])
    up_came, low_came = pair_b(up, False), pair_a(low, False)
    both = after_both_cores([up_came, low_came])
    up, low = pair_sum(up, low, up_came, low_came, [both])
    up_a, low_b = pair_a(up, True), pair_b(low, True)
    up_b, low_a = pair_b(up, True), pair_a(low, True)
    up_ab, low_ab = pair_b(up_a, True), pair_a(low_b, True)
    own = [[up, up_a, up_ab, up_b], [low, low_a, low_ab, low_b]]
    its = [[to_core(value) for value in values] for values in own]
    came = ((0, 0), (1, 0), (1, 1), (0, 1))
    blocks = [
        (values[low][n], low, values is own, *came[n])
        for values in (own, its)
        for n in (0, 1, 3, 2)
        for low in (0, 1)
    ]
    late = [block for block in blocks if block[3:] == (1, 1)]
    begun = write([block for block in blocks if block[3:] != (1, 1)], None, None)
    done = write(late, begun, [own[0], its[0]])
    small1, small2 = jnp.swapaxes(done.small1, 0, 1), jnp.swapaxes(done.small2, 0, 1)
    return small1, done._point1, small2, done._point2


def solution(mesh):
    sharded = P(None, REPLICA, None, None, None)
    by_section = P(SECTION, None, None)
    return jax.shard_map(
        per_device,
        mesh=mesh,
        in_specs=(sharded, sharded) + (by_section,) * 4,
        out_specs=(by_section,) * 4,
        check_vma=False,
    )
```

```python
import functools
from types import SimpleNamespace

import jax
import jax.numpy as jnp
from jax import lax
from jax.experimental import pallas as pl
from jax.experimental.pallas import tpu as pltpu
from jax.sharding import PartitionSpec as P

BF = jnp.bfloat16
F32 = jnp.float32
SIDE = 12
ROWS = SIDE * SIDE
C = 1024
GROUPS = C // 128
LINE = SIDE * GROUPS
MICRO = 4
SECTIONS = 4
MAP1 = (SIDE + 2) * LINE
MAP2 = (SIDE + 4) * LINE
FLAT = SIDE * LINE
MIB = 1024 * 1024
SECTION = "section"
REPLICA = "replica"

ANY = pl.BlockSpec(memory_space=pl.ANY)
VM = pl.BlockSpec(memory_space=pltpu.VMEM)


def sigmoid(v):
    return 0.5 * jnp.tanh(0.5 * v) + 0.5


def slope(v):
    s = sigmoid(v)
    return s * (1.0 + v * (1.0 - s))


def widen_kernel(k_ref, wide):
    for g in range(GROUPS):
        wide[pl.ds(g, 9, stride=GROUPS), :] = k_ref[:, 128 * g : 128 * (g + 1)].astype(F32)


def clear_edges(field, dilation):
    size = dilation * LINE
    zero = jnp.zeros((size, 128), F32)
    field[pl.ds(0, size), :] = zero
    field[pl.ds(FLAT + size, size), :] = zero


def depthwise(field, wide, out, dilation, flip):
    taps = [wide[pl.ds(8 * (8 - t if flip else t), 8), :] for t in range(9)]

    def line(i, carry):
        seen = {}

        def at(p, j):
            if (p, j) not in seen:
                start = pl.multiple_of((i + p * dilation) * LINE + j * GROUPS, 8)
                seen[p, j] = field[pl.ds(start, 8), :]
            return seen[p, j]

        for j in range(SIDE):
            total = None
            for t in range(9):
                p, q = divmod(t, 3)
                col = j + (q - 1) * dilation
                if 0 <= col < SIDE:
                    term = taps[t] * at(p, col)
                    total = term if total is None else total + term
            out[pl.ds(pl.multiple_of(i * LINE + j * GROUPS, 8), 8), :] = total
        return carry

    lax.fori_loop(0, SIDE, line, 0)


def kernel_grad(field, grad, dilation):
    def line(i, sums):
        sums = list(sums)
        seen = {}

        def at(p, j):
            if (p, j) not in seen:
                start = pl.multiple_of((i + p * dilation) * LINE + j * GROUPS, 8)
                seen[p, j] = field[pl.ds(start, 8), :]
            return seen[p, j]

        for j in range(SIDE):
            here = grad[pl.ds(pl.multiple_of((i + dilation) * LINE + j * GROUPS, 8), 8), :]
            for t in range(9):
                p, q = divmod(t, 3)
                col = j + (q - 1) * dilation
                if 0 <= col < SIDE:
                    sums[t] = sums[t] + here * at(p, col)
        return tuple(sums)

    return lax.fori_loop(0, SIDE, line, tuple(jnp.zeros((8, 128), F32) for _ in range(9)))


def rows_to_map(field, base, p, g, value):
    field[pl.ds(base + 16 * p * GROUPS + g, 16, stride=GROUPS), :] = value


def map_to_rows(field, p, g):
    return field[pl.ds(16 * p * GROUPS + g, 16, stride=GROUPS), :]


def tiles(body):
    def step(p, carry):
        for g in range(GROUPS):
            body(p, g, pl.ds(pl.multiple_of(16 * p, 16), 16), pl.ds(128 * g, 128))
        return carry

    lax.fori_loop(0, ROWS // 16, step, 0)


def dot(a, b, dims):
    return lax.dot_general(a, b, (dims, ((), ())), preferred_element_type=F32)


def rows_type(n=ROWS):
    return jax.ShapeDtypeStruct((n, C), BF)


def map_type(n):
    return jax.ShapeDtypeStruct((n, 128), F32)


def call(body, ins, outs, scratch, limit, name, flops, size, aliases=None):
    flat, tree = jax.tree.flatten(ins)
    out_flat, out_tree = jax.tree.flatten(outs)

    def kernel(*refs):
        first, last = len(flat), len(flat) + len(out_flat)
        given = SimpleNamespace(**jax.tree.unflatten(tree, refs[:first]))
        made = SimpleNamespace(**jax.tree.unflatten(out_tree, refs[first:last]))
        body(given, made, refs[last:])

    def names(arrays):
        return jax.tree.leaves({n: jax.tree.map(lambda _: n, value) for n, value in arrays.items()})

    def specs(arrays):
        return [ANY if n.startswith("_") else VM for n in names(arrays)]

    found = pl.pallas_call(
        kernel,
        out_shape=out_flat,
        in_specs=specs(ins),
        out_specs=specs(outs),
        scratch_shapes=scratch,
        input_output_aliases={
            names(ins).index(a): names(outs).index(b) for a, b in (aliases or {}).items()
        },
        compiler_params=pltpu.CompilerParams(vmem_limit_bytes=limit * MIB),
        cost_estimate=pl.CostEstimate(flops=flops, bytes_accessed=size, transcendentals=0),
        name=name,
    )(*flat)
    return SimpleNamespace(**jax.tree.unflatten(out_tree, found))


class Copies:
    def __init__(self, sems):
        self.sems = sems
        self.count = 0

    def next(self):
        self.count += 1
        return self.sems.at[self.count - 1]

    def start(self, source, target):
        copy = pltpu.make_async_copy(source, target, self.next())
        copy.start()
        return copy

    def by_section(self, section, choices, target):
        sem = self.next()
        for s, source in choices.items():

            @pl.when(section == s)
            def _(source=source):
                pltpu.make_async_copy(source, target, sem).start()

        return pltpu.make_async_copy(target, target, sem)

    def by_core(self, core, value, on_zero, on_one):
        sem = self.next()

        @pl.when(core == 0)
        def _():
            pltpu.make_async_copy(value, on_zero, sem).start()

        @pl.when(core == 1)
        def _():
            pltpu.make_async_copy(value, on_one, sem).start()

        return pltpu.make_async_copy(value, value, sem)


def this_core():
    return lax.rem(lax.axis_index(REPLICA), 2)


def rows_scratch(n=ROWS):
    return pltpu.VMEM((n, C), BF)


def map_scratch(n):
    return pltpu.VMEM((n, 128), F32)


def pick(section, target, choices):
    if len(choices) == 1:
        return next(iter(choices.values()))
    for s, ref in choices.items():

        @pl.when(section == s)
        def _(ref=ref):
            target[...] = ref[...]

    return target


def forward_sections(moment):
    return [s for s in range(SECTIONS) if 0 <= moment - s < MICRO]


def forward_body(moment, ins, outs, scratch):
    xs, wide1, wide2, map1, map2, work, fv, sv, pv, sems, *own = scratch
    section = lax.axis_index(SECTION)
    core = this_core()
    slot = moment - section

    @pl.when((slot >= 0) & (slot < MICRO))
    def _():
        copies = Copies(sems)
        x_out = outs.x
        if moment < MICRO:
            get_x = pltpu.make_async_copy(ins._images.at[moment], xs, copies.next())
            pl.when(section == 0)(get_x.start)
        puts = []
        if own:
            w1, w2 = own
            gets = [copies.start(ins._p1, w1), copies.start(ins._p2, w2)]
        else:
            w1, w2 = ins.p1, ins.p2
        widen_kernel(ins.k1, wide1)
        widen_kernel(ins.k2, wide2)
        clear_edges(map1, 1)
        clear_edges(map2, 2)
        if moment < MICRO:
            pl.when(section == 0)(get_x.wait)
        came = {s: ins.came[s % 2] for s in forward_sections(moment) if s > 0}
        if moment < MICRO and moment > 0:
            came[0] = xs
            for s, ref in came.items():
                if s > 0:

                    @pl.when(section == s)
                    def _(ref=ref):
                        xs[...] = ref[...]

        xv = xs if moment < MICRO else pick(section, xs, came)
        if moment > 0:
            puts.append(copies.start(xv, outs._x))

        def enter(p, g, rows, cols):
            v = xv[rows, cols].astype(F32)
            rows_to_map(map1, LINE, p, g, v * sigmoid(v))

        tiles(enter)
        depthwise(map1, wide1, work, 1, False)

        def collect_first(p, g, rows, cols):
            fv[rows, cols] = map_to_rows(work, p, g).astype(BF)

        tiles(collect_first)
        if own:
            for get in gets:
                get.wait()
        puts.append(copies.start(map1, outs._map1))
        puts.append(copies.by_core(core, fv, outs._keep, outs._send))
        for n in range(4):
            cols = pl.ds(256 * n, 256)
            pre = dot(fv[...], w1[:, cols], ((1,), (0,)))
            pv[:, cols] = pre.astype(BF)
            hidden = (pre * sigmoid(pre)).astype(BF).astype(F32)
            for g in range(2):
                map2[pl.ds(2 * LINE + 2 * n + g, ROWS, stride=GROUPS), :] = hidden[
                    :, 128 * g : 128 * (g + 1)
                ]
        puts.append(copies.start(pv, outs._proj))
        puts.append(copies.start(map2, outs._map2))
        depthwise(map2, wide2, work, 2, False)

        def collect_second(p, g, rows, cols):
            sv[rows, cols] = map_to_rows(work, p, g).astype(BF)

        tiles(collect_second)
        puts.append(copies.by_core(core, sv, outs._send, outs._keep))

        @pl.when(section != SECTIONS - 1)
        def _():
            for n in range(4):
                cols = pl.ds(256 * n, 256)
                branch = dot(sv[...], w2[:, cols], ((1,), (0,)))
                x_out[:, cols] = (xv[:, cols].astype(F32) + branch).astype(BF)

        for put in puts:
            put.wait()


def forward(moment, images, came, k1, k2, p1, p2, after):
    ins = dict(k1=k1, k2=k2, came=came, _after=after)
    ins.update(dict(p1=p1, p2=p2) if moment > 0 else dict(_p1=p1, _p2=p2))
    outs = dict(
        x=rows_type(),
        _map1=map_type(MAP1),
        _map2=map_type(MAP2),
        _proj=rows_type(),
        _keep=rows_type(),
        _send=rows_type(),
    )
    if moment < MICRO:
        ins.update(_images=images)
    if moment > 0:
        outs.update(_x=rows_type())
    return call(
        functools.partial(forward_body, moment),
        ins,
        outs,
        [
            rows_scratch(),
            map_scratch(72),
            map_scratch(72),
            map_scratch(MAP1),
            map_scratch(MAP2),
            map_scratch(FLAT),
            rows_scratch(),
            rows_scratch(),
            rows_scratch(),
            pltpu.SemaphoreType.DMA((10,)),
            *([rows_scratch(C), rows_scratch(C)] if moment == 0 else []),
        ],
        8 if moment > 0 else 14,
        f"fwd{moment}",
        4 * ROWS * C * C,
        8 * MIB,
    )


def turn_body(ins, outs, scratch):
    for out, value in ((outs.p1, ins.p1), (outs.p2, ins.p2)):
        for n in range(4):
            for m in range(4):
                rows, cols = pl.ds(256 * n, 256), pl.ds(256 * m, 256)
                out[cols, rows] = value[rows, cols].T


def turned(p1, p2, after):
    square = rows_type(C)
    found = call(
        turn_body,
        dict(p1=p1, p2=p2, _after=after),
        dict(p1=square, p2=square),
        [],
        8,
        "turn",
        100 * MIB,
        8 * MIB,
    )
    return found.p1, found.p2


def backward_pairs(moment):
    found = []
    for section in range(SECTIONS):
        micro = moment - (2 * SECTIONS - 2) + section
        if 0 <= micro < MICRO:
            found.append((section, micro, micro + section))
    return found


def is_active(section, pairs):
    return functools.reduce(lambda a, b: a | b, [section == s for s, _, _ in pairs])


def backward_body(moment, ins, outs, scratch):
    gs, xs, ps, wide1, wide2, map1, map2, work, hv, sems = scratch
    pairs = backward_pairs(moment)
    section = lax.axis_index(SECTION)
    core = this_core()

    @pl.when(is_active(section, pairs))
    def _():
        copies = Copies(sems)
        g_out = outs.g
        top = [micro for s, micro, _ in pairs if s == SECTIONS - 1]
        if top:
            get_g = pltpu.make_async_copy(ins._cotangent.at[top[0]], gs, copies.next())
            pl.when(section == SECTIONS - 1)(get_g.start)
        parts = [pl.ds(QUARTER * n, QUARTER) for n in range(4)]
        get_p = copies.by_section(section, {s: ins._proj[when] for s, _, when in pairs}, ps)
        get_x = copies.by_section(section, {s: ins._x[when] for s, _, when in pairs if s > 0}, xs)
        widen_kernel(ins.k1, wide1)
        widen_kernel(ins.k2, wide2)
        clear_edges(map1, 1)
        clear_edges(map2, 2)
        came = {s: ins.came[s % 2] for s, _, _ in pairs if s < SECTIONS - 1}
        if top:
            pl.when(section == SECTIONS - 1)(get_g.wait)
            for s, ref in came.items():

                @pl.when(section == s)
                def _(ref=ref):
                    gs[...] = ref[...]

        gv = gs if top else pick(section, gs, came)
        for n in range(4):
            part = dot(gv[...], ins.p2[:, parts[n]], ((1,), (0,)))
            part = part.astype(BF).astype(F32)
            for g in range(2):
                map2[pl.ds(2 * LINE + 2 * n + g, ROWS, stride=GROUPS), :] = part[
                    :, 128 * g : 128 * (g + 1)
                ]
        puts = [copies.by_core(core, gv, outs._send, outs._keep)]
        puts.append(copies.start(map2, outs._map2))
        depthwise(map2, wide2, work, 2, True)
        get_p.wait()

        def collect_hidden(p, g, rows, cols):
            hv[rows, cols] = (map_to_rows(work, p, g) * slope(ps[rows, cols].astype(F32))).astype(BF)

        tiles(collect_hidden)
        puts.append(copies.by_core(core, hv, outs._keep, outs._send))
        for n in range(4):
            part = dot(hv[...], ins.p1[:, parts[n]], ((1,), (0,)))
            part = part.astype(BF).astype(F32)
            for g in range(2):
                map1[pl.ds(LINE + 2 * n + g, ROWS, stride=GROUPS), :] = part[
                    :, 128 * g : 128 * (g + 1)
                ]
        puts.append(copies.start(map1, outs._map1))

        @pl.when(section != 0)
        def _():
            get_x.wait()
            depthwise(map1, wide1, work, 1, True)

            def collect(p, g, rows, cols):
                back = map_to_rows(work, p, g) * slope(xs[rows, cols].astype(F32))
                g_out[rows, cols] = (gv[rows, cols].astype(F32) + back).astype(BF)

            tiles(collect)

        for put in puts:
            put.wait()


def backward(moment, cotangent, came, xs, projs, k1, k2, p1, p2, after):
    ins = dict(k1=k1, k2=k2, p1=p1, p2=p2, _x={}, _proj={}, _after=after, came=came)
    for s, micro, when in backward_pairs(moment):
        if s == SECTIONS - 1:
            ins.update(_cotangent=cotangent)
        if s > 0:
            ins["_x"][when] = xs[when]
        ins["_proj"][when] = projs[when]
    return call(
        functools.partial(backward_body, moment),
        ins,
        dict(
            g=rows_type(),
            _map2=map_type(MAP2),
            _map1=map_type(MAP1),
            _keep=rows_type(),
            _send=rows_type(),
        ),
        [
            rows_scratch(),
            rows_scratch(),
            rows_scratch(),
            map_scratch(72),
            map_scratch(72),
            map_scratch(MAP1),
            map_scratch(MAP2),
            map_scratch(FLAT),
            rows_scratch(),
            pltpu.SemaphoreType.DMA((12,)),
        ],
        8,
        f"bwd{moment}",
        4 * ROWS * C * C,
        8 * MIB,
    )


def taps_body(moment, ins, outs, scratch):
    s1, s2, g1, g2, sems = scratch
    out = outs.sums
    pairs = backward_pairs(moment)
    section = lax.axis_index(SECTION)
    active = is_active(section, pairs)

    @pl.when(active)
    def _():
        copies = Copies(sems)
        get = [copies.by_section(section, {s: ins._s2[when] for s, _, when in pairs}, s2)]
        get.append(copies.start(ins._g2, g2))
        later = [copies.by_section(section, {s: ins._s1[when] for s, _, when in pairs}, s1)]
        later.append(copies.start(ins._g1, g1))
        for start, field, grad, dilation, waits in ((9, s2, g2, 2, get), (0, s1, g1, 1, later)):
            for copy in waits:
                copy.wait()
            found = kernel_grad(field, grad, dilation)
            for t in range(9):
                rows = pl.ds(8 * (start + t), 8)
                out[rows, :] = found[t] + (ins.sums[rows, :] if moment > SECTIONS - 1 else 0.0)

    @pl.when(jnp.logical_not(active))
    def _():
        out[...] = ins.sums[...] if moment > SECTIONS - 1 else jnp.zeros_like(out)


def taps(moment, sums, maps1, maps2, g1, g2, after):
    ins = dict(_g1=g1, _g2=g2, _s1={}, _s2={}, _after=after)
    if sums is not None:
        ins.update(sums=sums)
    for s, micro, when in backward_pairs(moment):
        ins["_s1"][when] = maps1[when]
        ins["_s2"][when] = maps2[when]
    return call(
        functools.partial(taps_body, moment),
        ins,
        dict(sums=map_type(18 * GROUPS)),
        [
            map_scratch(MAP1),
            map_scratch(MAP2),
            map_scratch(MAP1),
            map_scratch(MAP2),
            pltpu.SemaphoreType.DMA((4,)),
        ],
        6,
        f"taps{moment}",
        40 * ROWS * C,
        3 * MIB,
    ).sums


QUARTER = C // 4
HALF = QUARTER // 2
SMALL = 16


def places():
    replica = lax.axis_index(REPLICA)
    core = lax.rem(replica, 2)
    x = lax.rem(lax.div(replica, 2), 4)
    y = lax.div(replica, 8)
    return core, jnp.where(core == 0, x, y), jnp.where(core == 0, y, x)


def gather_operands(operands, micros):
    ahead = [m + s for m in micros for s in range(SECTIONS)]
    back = [m + 2 * SECTIONS - 2 - s for m in micros for s in range(SECTIONS)]
    left = [{t: value[t] for t in ahead} for value in operands[:2]]
    right = [{t: value[t] for t in back} for value in operands[2:]]
    return dict(_lefts=left, _rights=right)


def stack_operands(ins, micros, left, right, sems):
    section = lax.axis_index(SECTION)
    for s in range(SECTIONS):

        @pl.when(section == s)
        def _(s=s):
            for n, m in enumerate(micros):
                ahead, back = m + s, m + 2 * SECTIONS - 2 - s
                for h in range(2):
                    k = 2 * n + h
                    rows = pl.ds(k * ROWS, ROWS)
                    a, b = ins._lefts[h][ahead], ins._rights[h][back]
                    pltpu.make_async_copy(a, left.at[rows, :], sems.at[2 * k]).start()
                    pltpu.make_async_copy(b, right.at[rows, :], sems.at[2 * k + 1]).start()

    for k in range(2 * len(micros)):
        rows = pl.ds(k * ROWS, ROWS)
        pltpu.make_async_copy(left.at[rows, :], left.at[rows, :], sems.at[2 * k]).wait()
        pltpu.make_async_copy(right.at[rows, :], right.at[rows, :], sems.at[2 * k + 1]).wait()


def early_body(micros, ins, outs, scratch):
    left, right, sems = scratch
    out = outs.early
    stack_operands(ins, micros, left, right, sems)

    def part(n, carry):
        start = pl.multiple_of(n * QUARTER, QUARTER)
        out[pl.ds(start, QUARTER), :] = dot(left[:, pl.ds(start, QUARTER)], right[...], ((0,), (0,)))
        return carry

    lax.fori_loop(0, 4, part, 0)


def early_weights(operands):
    micros = tuple(range(MICRO - 1))
    size = 2 * len(micros) * ROWS
    return call(
        functools.partial(early_body, micros),
        gather_operands(operands, micros),
        dict(early=jax.ShapeDtypeStruct((C, C), F32)),
        [rows_scratch(size), rows_scratch(size), pltpu.SemaphoreType.DMA((4 * len(micros),))],
        12,
        "early_weights",
        2 * size * C * C,
        8 * MIB,
    ).early


def part_of(early, left, right, number):
    start = pl.multiple_of(lax.rem(number, 4) * QUARTER, QUARTER)
    added = dot(left[:, pl.ds(start, QUARTER)], right[...], ((0,), (0,)))
    return early[pl.ds(start, QUARTER), :] + added


def far_body(ins, outs, scratch):
    (sems,) = scratch
    left, right = outs.left, outs.right
    stack_operands(ins, (MICRO - 1,), left, right, sems)
    _, mine, _ = places()
    whole = part_of(ins.early, left, right, mine + 2).astype(BF)
    outs.up[...] = whole[:HALF]
    outs.low[...] = whole[HALF:]


def far_part(operands, early):
    size = 2 * ROWS
    return call(
        far_body,
        dict(early=early, **gather_operands(operands, (MICRO - 1,))),
        dict(
            up=rows_type(HALF),
            low=rows_type(HALF),
            left=rows_type(size),
            right=rows_type(size),
        ),
        [pltpu.SemaphoreType.DMA((4,))],
        8,
        "far_part",
        2 * size * C * QUARTER,
        3 * MIB,
    )


def tail_body(ins, outs, scratch):
    small, wide = scratch
    both = ins.sums[...] + ins.other[...]
    small[...] = jnp.where(this_core() == 0, both[:72], both[72:])
    wide[...] = jnp.zeros((SMALL, C), F32)
    for g in range(GROUPS):
        wide[pl.ds(0, 9), 128 * g : 128 * (g + 1)] = small[pl.ds(g, 9, stride=GROUPS), :]
    outs.tail[...] = wide[...].astype(BF)


def tail_part(sums, other):
    return call(
        tail_body,
        dict(sums=sums, other=other),
        dict(tail=rows_type(SMALL)),
        [map_scratch(72), pltpu.VMEM((SMALL, C), F32)],
        2,
        "tail",
        0,
        MIB,
    ).tail


def near_body(ins, outs, scratch):
    _, mine, _ = places()
    after = part_of(ins.early, ins.left, ins.right, mine + 1)
    outs.after_up[...] = after[:HALF]
    outs.after_low[...] = after[HALF:].astype(BF)
    before = part_of(ins.early, ins.left, ins.right, mine + 3)
    outs.before_up[...] = before[:HALF].astype(BF)
    outs.before_low[...] = before[HALF:]
    outs.own[...] = part_of(ins.early, ins.left, ins.right, mine)


def wide_type(n):
    return jax.ShapeDtypeStruct((n, C), F32)


def near_parts(early, left, right):
    return call(
        near_body,
        dict(early=early, left=left, right=right),
        dict(
            after_up=wide_type(HALF),
            after_low=rows_type(HALF),
            before_up=rows_type(HALF),
            before_low=wide_type(HALF),
            own=wide_type(QUARTER),
        ),
        [],
        8,
        "near_parts",
        2 * 2 * ROWS * C * QUARTER * 3,
        8 * MIB,
    )


def relay_body(ins, outs, scratch):
    outs.after[...] = (ins.after[...] + ins.up[...].astype(F32)).astype(BF)
    outs.before[...] = (ins.before[...] + ins.low[...].astype(F32)).astype(BF)


def relay(after, before, up, low, waits):
    return call(
        relay_body,
        dict(after=after, before=before, up=up, low=low, _after=waits),
        dict(after=rows_type(HALF), before=rows_type(HALF)),
        [],
        4,
        "relay",
        0,
        4 * MIB,
    )


def mark_body(ins, outs, scratch):
    outs.mark[...] = jnp.zeros_like(outs.mark)


def after_both_cores(values):
    mark = call(mark_body, dict(_after=values), dict(mark=map_type(8)), [], 1, "mark", 0, 4096).mark
    return to_core(mark)


def ring_sum(a, b, c, d):
    a, b, c, d = (value.astype(F32) for value in (a, b, c, d))
    return (a + b) + (c + d)


def first_sum_body(ins, outs, scratch):
    up, low = [a.astype(F32) + b.astype(F32) for a, b in ((ins.ups[0][...], ins.ups[1][...]), (ins.lows[0][...], ins.lows[1][...]))]
    outs.up[pl.ds(0, HALF), :] = (ins.own[:HALF] + up).astype(BF)
    outs.up[pl.ds(HALF, SMALL), :] = ins.tail[...]
    outs.low[...] = (ins.own[HALF:] + low).astype(BF)


def first_sum(own, ups, lows, tail, waits):
    found = call(
        first_sum_body,
        dict(own=own, ups=ups, lows=lows, tail=tail, _after=waits),
        dict(up=rows_type(HALF + SMALL), low=rows_type(HALF)),
        [],
        4,
        "first_sum",
        0,
        4 * MIB,
    )
    return found.up, found.low


def pair_sum_body(ins, outs, scratch):
    outs.up[...] = (ins.up[...].astype(F32) + ins.up_came[...].astype(F32)).astype(BF)
    outs.low[...] = (ins.low[...].astype(F32) + ins.low_came[...].astype(F32)).astype(BF)


def pair_sum(up, low, up_came, low_came, waits):
    found = call(
        pair_sum_body,
        dict(up=up, low=low, up_came=up_came, low_came=low_came, _after=waits),
        dict(up=rows_type(HALF + SMALL), low=rows_type(HALF)),
        [],
        3,
        "pair_sum",
        0,
        2 * MIB,
    )
    return found.up, found.low


def other_a(place):
    return place + 1 - 2 * lax.rem(place, 2)


def other_b(place):
    return 3 - place


def convert(outs, blocks, wide, sems):
    core, mine, its = places()
    waits = []
    for n, (part, low, own, by_a, by_b) in enumerate(blocks):
        place = mine if own else its
        place = other_a(place) if by_a else place
        place = other_b(place) if by_b else place
        slot, sem = wide.at[n], sems.at[n]
        slot[...] = part[pl.ds(0, HALF), :].astype(F32)
        rows = pl.ds(pl.multiple_of(place * QUARTER + low * HALF, HALF), HALF)

        @pl.when(core == (0 if own else 1))
        def _(slot=slot, rows=rows, sem=sem):
            pltpu.make_async_copy(slot, outs._point1.at[0, rows, :], sem).start()

        @pl.when(core == (1 if own else 0))
        def _(slot=slot, rows=rows, sem=sem):
            pltpu.make_async_copy(slot, outs._point2.at[0, rows, :], sem).start()

        waits.append(pltpu.make_async_copy(slot, slot, sem))
    for copy in waits:
        copy.wait()


POINT = jax.ShapeDtypeStruct((1, C, C), F32)


def write_body(kinds, with_tails, ins, outs, scratch):
    if with_tails:
        own, its = [
            ring_sum(*[ins.tails[n][k][pl.ds(HALF, SMALL), :] for k in range(4)])[:9] for n in range(2)
        ]
        core = this_core()
        outs.small1[:, 0, :] = jnp.where(core == 0, own, its)
        outs.small2[:, 0, :] = jnp.where(core == 0, its, own)
    convert(outs, [(ins.parts[n], *kind) for n, kind in enumerate(kinds)], *scratch)


def write(blocks, begun, tails):
    parts = [block[0] for block in blocks]
    ins, outs = dict(parts=parts), dict(_point1=POINT, _point2=POINT)
    aliases = None
    if begun is not None:
        ins.update(_was1=begun._point1, _was2=begun._point2)
        aliases = dict(_was1="_point1", _was2="_point2")
    if tails:
        small = jax.ShapeDtypeStruct((9, 1, C), F32)
        ins.update(tails=tails)
        outs.update(small1=small, small2=small)
    return call(
        functools.partial(write_body, [block[1:] for block in blocks], bool(tails)),
        ins,
        outs,
        [pltpu.VMEM((len(blocks), HALF, C), F32), pltpu.SemaphoreType.DMA((len(blocks),))],
        10,
        "write",
        100 * MIB,
        len(blocks) * HALF * C * 6,
        aliases,
    )


def to_replica(value, target):
    return lax.ppermute(value, REPLICA, [(r, target(r)) for r in range(32)])


def to_core(value):
    return to_replica(value, lambda r: r ^ 1)


def along_x(r, d):
    return (r // 8) * 8 + ((r // 2 + d) % 4) * 2 + r % 2


def along_y(r, d):
    return ((r // 8 + d) % 4) * 8 + r % 8


def along_first(value, d):
    return to_replica(value, lambda r: along_x(r, d) if r % 2 == 0 else along_y(r, d))


def pair_a(value, first):
    return to_pair(value, first, lambda place: place ^ 1)


def pair_b(value, first):
    return to_pair(value, first, lambda place: 3 - place)


def to_pair(value, first, partner):
    def target(r):
        x, y, core = (r // 2) % 4, r // 8, r % 2
        if (core == 0) == first:
            x = partner(x)
        else:
            y = partner(y)
        return y * 8 + x * 2 + core

    return to_replica(value, target)


def to_neighbours(value, pairs, step, swap):
    came = {}
    for source, target in pairs:
        near = min(source, target) % 2 == 0
        if target % 2 not in came and swap:
            places = [(s, s ^ 1 if near else 3 - s) for s in range(SECTIONS)]
            came[target % 2] = lax.ppermute(value, SECTION, places)
    if pairs and not swap:
        places = [(s, s + step) for s in range(SECTIONS) if 0 <= s + step < SECTIONS]
        came[0] = came[1] = lax.ppermute(value, SECTION, places)
    return came


def per_device(images, cotangent, depth_first, point_first, depth_second, point_second):
    images = images.reshape(MICRO, ROWS, C)
    cotangent = cotangent.reshape(MICRO, ROWS, C)
    weights = (depth_first[0], depth_second[0], point_first[0], point_second[0])
    xs, projs, maps1, maps2 = {}, {}, {}, {}
    operands = ({}, {}, {}, {})
    grads1, grads2 = {}, {}
    came, returned = {}, {}
    sums = early = None
    last = 3 * SECTIONS - 3
    full = MICRO + SECTIONS - 2
    for moment in range(last + 1):
        if moment <= full:
            after = [operands[1][moment - 2]] if 1 < moment < MICRO else []
            if moment == 2:
                after += back_weights[2:]
            found = forward(moment, images, came, *weights, after)
            maps1[moment], maps2[moment] = found._map1, found._map2
            projs[moment] = found._proj
            if moment > 0:
                xs[moment] = found._x
            operands[0][moment] = found._keep
            if moment == 0:
                back_weights = [*weights[:2], *turned(*weights[2:], [found._keep])]
            operands[1][moment] = to_core(found._send)
            going = [(s, s + 1) for s in forward_sections(moment) if s < SECTIONS - 1]
            came = to_neighbours(found.x, sorted(going, reverse=True), 1, moment < SECTIONS - 1)
        if moment >= SECTIONS - 1:
            after = [] if sums is None else [sums]
            after += [] if early is None else [early]
            if moment == full + 1:
                after += [operands[1][past] for past in range(MICRO - 2, full + 1)]
            if moment == full + 2:
                after += [operands[3][past] for past in range(SECTIONS - 1, full + 1)]
            found = backward(moment, cotangent, returned, xs, projs, *back_weights, after)
            grads2[moment], grads1[moment] = found._map2, found._map1
            operands[2][moment] = found._keep
            operands[3][moment] = to_core(found._send)
            going = [(s, s - 1) for s, _, _ in backward_pairs(moment) if s > 0]
            returned = to_neighbours(found.g, sorted(going, reverse=True), -1, moment >= full)
        if full <= moment < last:
            for past in range(SECTIONS - 1, moment + 1) if moment == full else [moment]:
                sums = taps(past, sums, maps1, maps2, grads1[past], grads2[past], [grads1[moment]])
        if moment == last - 1:
            early = early_weights(operands)
    far = far_part(operands, early)
    up, low = along_first(far.up, 1), along_first(far.low, -1)
    near = near_parts(early, far.left, far.right)
    near_low, near_up = along_first(near.after_low, 1), along_first(near.before_up, -1)
    sent = relay(near.after_up, near.before_low, up, low, [])
    sums = taps(last, sums, maps1, maps2, grads1[last], grads2[last], [sent.after])
    tail = tail_part(sums, to_core(sums))
    up, low = along_first(sent.after, 1), along_first(sent.before, -1)
    up, low = first_sum(near.own, [up, near_up], [near_low, low], tail, [])
    up, low = pair_sum(up, low, pair_a(up, False), pair_b(low, False), [])
    up_came, low_came = pair_b(up, False), pair_a(low, False)
    both = after_both_cores([up_came, low_came])
    up, low = pair_sum(up, low, up_came, low_came, [both])
    up_a, low_b = pair_a(up, True), pair_b(low, True)
    up_b, low_a = pair_b(up, True), pair_a(low, True)
    up_ab, low_ab = pair_b(up_a, True), pair_a(low_b, True)
    own = [[up, up_a, up_ab, up_b], [low, low_a, low_ab, low_b]]
    its = [[to_core(value) for value in values] for values in own]
    came = ((0, 0), (1, 0), (1, 1), (0, 1))
    blocks = [
        (values[low][n], low, values is own, *came[n])
        for values in (own, its)
        for n in (0, 1, 3, 2)
        for low in (0, 1)
    ]
    late = [block for block in blocks if block[3:] == (1, 1)]
    begun = write([block for block in blocks if block[3:] != (1, 1)], None, None)
    done = write(late, begun, [own[0], its[0]])
    small1, small2 = jnp.swapaxes(done.small1, 0, 1), jnp.swapaxes(done.small2, 0, 1)
    return small1, done._point1, small2, done._point2


def solution(mesh):
    sharded = P(None, REPLICA, None, None, None)
    by_section = P(SECTION, None, None)
    return jax.shard_map(
        per_device,
        mesh=mesh,
        in_specs=(sharded, sharded) + (by_section,) * 4,
        out_specs=(by_section,) * 4,
        check_vma=False,
    )
```
